256 devices in a mesh: seq: 32 (over z_lo, x, core), heads: 8 (over z_hi, y).
Axes of the slice: x: 4, y: 4, z: 8 (z_hi: 2, z_lo: 4; z = z_hi * 4 + z_lo), core: 2. Of those that a mesh axis runs over, the one named last changes fastest.
Arguments:
- query_rows: bfloat16 [4096, 8192], P('seq', 'heads'), may hold values from -128 to 128
- key_rows: bfloat16 [4096, 1024], P('seq', 'heads'), may hold values from -8 to 8
- value_rows: bfloat16 [4096, 1024], P('seq', 'heads'), may hold values from -6 to 6
- out_grad: bfloat16 [4096, 8192], P('seq', 'heads'), may hold values from -6 to 6
- log_ratio: float32 [4096], P(('seq', 'heads')), may hold values from -12 to 12
- block_mask: int32 [32, 32], replicated, may hold values from 0 to 1, as said below
- response_bounds: int32 [9], replicated, may hold values from 128 to 4096, as said below
- pair_index: int32 [8, 2], replicated, may hold values from 0 to 7, all different within a row
Outputs:
- query_grad: bfloat16 [4096, 8192], P('seq', 'heads')
- key_grad: bfloat16 [4096, 1024], P('seq', 'heads')
- value_grad: bfloat16 [4096, 1024], P('seq', 'heads')
The draws below stay inside these ranges and needn't reach their ends.
Inputs may be any that keep to these rules, and one draw needn't show every extreme that they name: block_mask[i, j] is 1 exactly where j <= i and block j lies in the prompt or in the same response as block i, as given by response_bounds. response_bounds[0] ends the prompt and response r covers positions response_bounds[r] to response_bounds[r+1] - 1; all are multiples of 128, strictly rising, the prompt is at least one block and the last entry is 4096. `pair_index`: each row names two different responses, preferred first.
All inputs are finite; a program needn't handle non-finite values.
Results may differ from the reference program's by a relative error of at most 0.039.
Values may be sent and summed in bfloat16 or wider, within the bound.
No kernel may reach another device: no remote copies, remote signals or barrier semaphores. Data moves between devices by JAX's collectives and lax.ppermute only.
A program may use at most 64 MiB of HBM per device.

```python
import math
import jax
import jax.numpy as jnp
from jax import lax

DH = 128
HQ = 64
KVH = 8
BLOCK = 128
RESP = 8
PAIRS = 8
TOKENS = 4096


def layout(key):
    nblocks = TOKENS // BLOCK
    prompt = jax.random.randint(jax.random.fold_in(key, 101), (), nblocks // 8, nblocks // 4 + 1)
    ranking = jax.random.permutation(jax.random.fold_in(key, 102), nblocks).astype(jnp.int32)
    block_ids = jnp.arange(nblocks, dtype=jnp.int32)
    ranked = jnp.where(block_ids > prompt, ranking + 1, -block_ids - 1)
    chosen = lax.top_k(ranked, RESP - 1)[1].astype(jnp.int32)
    cut_blocks = jnp.sort(chosen)
    return jnp.concatenate([prompt.reshape(1).astype(jnp.int32), cut_blocks, jnp.full((1,), nblocks, jnp.int32)])


def shared_keys(key):
    return jnp.clip(jax.random.normal(jax.random.fold_in(key, 201), (TOKENS, KVH * DH), jnp.float32), -6.0, 6.0)


def draw_response_bounds(key, part):
    bound_blocks = layout(key)
    return (bound_blocks * BLOCK).astype(jnp.int32)


def draw_block_mask(key, part):
    bound_blocks = layout(key)
    nblocks = TOKENS // BLOCK
    block_ids = jnp.arange(nblocks, dtype=jnp.int32)
    resp_of = jnp.sum((block_ids[:, None] >= bound_blocks[None, :RESP]).astype(jnp.int32), axis=1) - 1
    causal = block_ids[None, :] <= block_ids[:, None]
    allowed = (resp_of[None, :] == -1) | (resp_of[None, :] == resp_of[:, None])
    return (causal & allowed).astype(jnp.int32)


def draw_key_rows(key, part):
    base_keys = shared_keys(key)
    return base_keys.astype(jnp.bfloat16)


def draw_query_rows(key, part):
    key = jax.random.fold_in(key, 3)
    queries = jnp.clip(jax.random.normal(key, (TOKENS, HQ * DH), jnp.float32), -6.0, 6.0)
    return queries.astype(jnp.bfloat16)


def block_scale(key, shape, pieces, least, largest):
    def one(position, parts):
        steps = jax.random.uniform(jax.random.fold_in(jax.random.fold_in(key, 6), position), (parts,), jnp.float32, least / len(pieces), largest / len(pieces))
        return jnp.repeat(jnp.exp(steps), shape[position] // parts).reshape((-1,) + (1,) * (len(shape) - position - 1))

    gain = one(*pieces[0])
    for cut in pieces[1:]:
        gain = gain * one(*cut)
    return gain


def different_ones(stream_key, rows, count, top, lift):
    order = jax.random.permutation(jax.random.fold_in(stream_key, 1), count)
    favour = order
    for power in range(3):
        favour = favour * favour // count
    favour = favour * lift // count
    chance = jax.random.randint(jax.random.fold_in(stream_key, 2), (rows, count), 0, 4096) + favour
    fixed_rows = jax.random.permutation(jax.random.fold_in(stream_key, 3), rows)[jnp.arange(count) % rows]
    chance = jnp.where(jnp.arange(rows)[:, None] == fixed_rows[None, :], 1 << 14, chance)
    score = chance * count + jnp.arange(count)
    return lax.top_k(score.astype(jnp.int32), top)[1].astype(jnp.int32)


def centred(rng, dims, width, limit, pieces=(), held_as=jnp.bfloat16):
    level = block_scale(rng, dims, pieces, -0.22, 0.18) if pieces else 1.0
    array = jax.random.normal(rng, dims, jnp.float32) * width * level
    return jnp.minimum(jnp.maximum(array, -limit), limit).astype(held_as)


def setup_inputs(seed: int = 0) -> dict:
    splits = jax.random.split(jax.random.key(seed), 9)
    query_rows = draw_query_rows(jax.random.fold_in(splits[8], 71), 0)
    key_rows = draw_key_rows(jax.random.fold_in(splits[8], 71), 0)
    value_rows = centred(splits[2], (TOKENS, KVH * DH), 1.0, 6.0, ((0, 32), (1, 8)))
    out_grad = centred(splits[3], (TOKENS, HQ * DH), 1.0, 6.0, ((0, 32), (1, 8)))
    log_ratio = centred(splits[4], (TOKENS,), 3.0, 12.0, ((0, 256),), jnp.float32)
    block_mask = draw_block_mask(jax.random.fold_in(splits[8], 71), 0)
    response_bounds = draw_response_bounds(jax.random.fold_in(splits[8], 71), 0)
    pair_index = different_ones(splits[7], PAIRS, RESP, 2, 0)
    return dict(query_rows=query_rows, key_rows=key_rows, value_rows=value_rows, out_grad=out_grad, log_ratio=log_ratio, block_mask=block_mask, response_bounds=response_bounds, pair_index=pair_index)


loss_scale = 512.0
margin_target = 1.0

def response_sums(ratios, positions, starts, resp_ends):
    member = (positions[None, :] >= starts[:, None]) & (positions[None, :] < resp_ends[:, None])
    return lax.optimization_barrier(jnp.sum(jnp.where(member, ratios[None, :], 0.0), axis=1))

def coefficients(means, pair_index):
    resp_ids = jnp.arange(RESP, dtype=jnp.int32)
    winner = (pair_index[:, 0:1] == resp_ids[None, :]).astype(jnp.float32)
    loser = (pair_index[:, 1:2] == resp_ids[None, :]).astype(jnp.float32)
    margin = lax.optimization_barrier(jnp.sum(winner * means[None, :], axis=1)) - lax.optimization_barrier(jnp.sum(loser * means[None, :], axis=1))
    resid = margin - margin_target
    return 2.0 / PAIRS * lax.optimization_barrier(jnp.sum(resid[:, None] * (winner - loser), axis=0))

def head_grads(query_head, key_head, value_head, grad_head, block_mask):
    block_rows = math.gcd(512, TOKENS)
    score_scale = 1.0 / math.sqrt(DH)
    key_f = key_head.astype(jnp.float32)
    value_f = value_head.astype(jnp.float32)
    key_pos = jnp.arange(TOKENS, dtype=jnp.int32)

    def block_step(carry, block_index):
        key_acc, value_acc = carry
        first_row = block_index * block_rows
        query_blk = lax.dynamic_slice_in_dim(query_head, first_row, block_rows, 0).astype(jnp.float32)
        grad_blk = lax.dynamic_slice_in_dim(grad_head, first_row, block_rows, 0).astype(jnp.float32)
        query_pos = first_row + jnp.arange(block_rows, dtype=jnp.int32)
        seen = block_mask[(query_pos // BLOCK)[:, None], (key_pos // BLOCK)[None, :]] == 1
        is_live = seen & (key_pos[None, :] <= query_pos[:, None])
        scores = jnp.einsum('tgd,nd->gtn', query_blk, key_f) * score_scale
        scores = jnp.where(is_live[None], scores, -jnp.inf)
        row_max = lax.optimization_barrier(jnp.max(scores, axis=-1))
        probs = jnp.exp(scores - row_max[..., None])
        row_sum = lax.optimization_barrier(jnp.sum(probs, axis=-1))
        attn_weights = lax.optimization_barrier(probs.astype(jnp.bfloat16)).astype(jnp.float32)
        attn_out = (jnp.einsum('gtn,nd->gtd', attn_weights, value_f) / row_sum[..., None]).astype(jnp.bfloat16)
        log_norm = row_max + jnp.log(row_sum)
        grad_t = jnp.transpose(grad_blk, (1, 0, 2))
        row_delta = lax.optimization_barrier(jnp.sum(grad_t * attn_out.astype(jnp.float32), axis=-1))
        prob_f = lax.optimization_barrier(jnp.exp(scores - log_norm[..., None]).astype(jnp.bfloat16)).astype(jnp.float32)
        grad_prob = jnp.einsum('gtd,nd->gtn', grad_t, value_f)
        grad_score = lax.optimization_barrier((prob_f * (grad_prob - row_delta[..., None])).astype(jnp.bfloat16)).astype(jnp.float32)
        query_grad = jnp.einsum('gtn,nd->tgd', grad_score, key_f) * score_scale
        key_acc = key_acc + jnp.einsum('gtn,gtd->nd', grad_score, jnp.transpose(query_blk, (1, 0, 2))) * score_scale
        value_acc = value_acc + jnp.einsum('gtn,gtd->nd', prob_f, grad_t)
        return ((key_acc, value_acc), query_grad)
    zeros_acc = jnp.zeros((TOKENS, DH), jnp.float32)
    (key_acc, value_acc), query_grad = lax.scan(block_step, (zeros_acc, zeros_acc), jnp.arange(TOKENS // block_rows, dtype=jnp.int32))
    return (query_grad.reshape(TOKENS, HQ // KVH, DH), key_acc, value_acc)

def reference(query_rows, key_rows, value_rows, out_grad, log_ratio, block_mask, response_bounds, pair_index):
    group_size = HQ // KVH
    positions = jnp.arange(TOKENS, dtype=jnp.int32)
    starts = response_bounds[:RESP]
    resp_ends = response_bounds[1:]
    lengths = (resp_ends - starts).astype(jnp.float32)
    resp_sums = response_sums(log_ratio, positions, starts, resp_ends)
    coef_resp = coefficients(resp_sums / lengths, pair_index)
    member = (positions[None, :] >= starts[:, None]) & (positions[None, :] < resp_ends[:, None])
    weight = lax.optimization_barrier(jnp.sum(jnp.where(member, (coef_resp / lengths)[:, None], 0.0), axis=0))
    grad_out = (weight[:, None] * out_grad.astype(jnp.float32) * loss_scale).astype(jnp.bfloat16)
    query_heads = jnp.transpose(query_rows.reshape(TOKENS, KVH, group_size, DH), (1, 0, 2, 3))
    grad_heads = jnp.transpose(grad_out.reshape(TOKENS, KVH, group_size, DH), (1, 0, 2, 3))
    key_heads = jnp.transpose(key_rows.reshape(TOKENS, KVH, DH), (1, 0, 2))
    value_heads = jnp.transpose(value_rows.reshape(TOKENS, KVH, DH), (1, 0, 2))
    query_grad, key_grad, value_grad = lax.map(lambda args: head_grads(args[0], args[1], args[2], args[3], block_mask), (query_heads, key_heads, value_heads, grad_heads))
    query_grad = jnp.transpose(query_grad, (1, 0, 2, 3)).reshape(TOKENS, HQ * DH).astype(jnp.bfloat16)
    key_grad = jnp.transpose(key_grad, (1, 0, 2)).reshape(TOKENS, KVH * DH).astype(jnp.bfloat16)
    value_grad = jnp.transpose(value_grad, (1, 0, 2)).reshape(TOKENS, KVH * DH).astype(jnp.bfloat16)
    return (query_grad, key_grad, value_grad)
```

```python
import math

import jax
import jax.numpy as jnp
from jax import lax
from jax.experimental import pallas as pl
from jax.experimental.pallas import tpu as pltpu
from jax.sharding import PartitionSpec as P

DH=128; BLOCK=128; RESP=8; GROUP=8
ROWS=GROUP*BLOCK
scale=1.0/math.sqrt(DH)
c2=scale*math.log2(math.e)
f32=jnp.float32; bf=jnp.bfloat16
NT=(((1,),(1,)),((),())); NN=(((1,),(0,)),((),()))
NB=4
KC=NB*BLOCK
W=1024
NCH=32//NB

def attend_body(me, bounds, q_ref, do_ref, bufs, dq_ref, keep_ref, send_ref, kk, vv, q2, g2, pb, dp_s, mt, mx, sm, dl, acc, sem):
    prompt = bounds[0]//BLOCK
    start = jnp.int32(0)
    for r in range(RESP):
        lo=bounds[r]//BLOCK
        start=jnp.where(me>=lo, lo, start)
    live = me>=prompt
    n = jnp.where(live, prompt + me - start + 1, 0)
    chunks = (n+NB-1)//NB
    z=me//8; x=(me//2)%4; c=me%2
    def where_is(t):
        j=jnp.where(t<prompt, t, start+t-prompt)
        return lax.rem(lax.rem(j,2)+c,2)*4 + lax.rem(x-lax.rem(j//2,4)+4,4), lax.rem(z-j//8+4,4)
    def fetch(t,_):
        b,sz=where_is(t)
        rows=pl.ds(pl.multiple_of(t*BLOCK,BLOCK),BLOCK)
        for nb,buf in enumerate(bufs):
            @pl.when(b==nb)
            def _(buf=buf):
                pltpu.make_async_copy(buf.at[sz,0],kk.at[rows],sem.at[0,t]).start()
                pltpu.make_async_copy(buf.at[sz,1],vv.at[rows],sem.at[1,t]).start()
        return 0
    lax.fori_loop(0,n,fetch,0)
    for h in range(GROUP):
        q2[h*128:(h+1)*128,:]=q_ref[:,h*128:(h+1)*128]
        g2[h*128:(h+1)*128,:]=do_ref[:,h*128:(h+1)*128]
    keep_ref[...]=jnp.zeros_like(keep_ref)
    send_ref[...]=jnp.zeros_like(send_ref)
    mx[...]=jnp.full_like(mx,-1e30)
    sm[...]=jnp.zeros_like(sm); dl[...]=jnp.zeros_like(dl)
    acc[...]=jnp.zeros_like(acc)
    def pad(t,_):
        rows=pl.ds(pl.multiple_of(t*BLOCK,BLOCK),BLOCK)
        kk[rows,:]=jnp.zeros((BLOCK,DH),bf); vv[rows,:]=jnp.zeros((BLOCK,DH),bf)
        return 0
    lax.fori_loop(n,chunks*NB,pad,0)
    def land(t,_):
        rows=pl.ds(pl.multiple_of(t*BLOCK,BLOCK),BLOCK)
        pltpu.make_async_copy(bufs[0].at[0,0],kk.at[rows],sem.at[0,t]).wait()
        pltpu.make_async_copy(bufs[0].at[0,1],vv.at[rows],sem.at[1,t]).wait()
        return 0
    lax.fori_loop(0,n,land,0)
    def forward(i,masked):
        rows=pl.ds(pl.multiple_of(i*KC,KC),KC)
        k=kk[rows,:]; v=vv[rows,:]
        def tile(w,_):
            sl=slice(w*W,(w+1)*W)
            s=lax.dot_general(k,q2[sl,:],NT,preferred_element_type=f32)*c2
            if masked:
                key=lax.broadcasted_iota(jnp.int32,(KC,W),0)+i*KC-(n-1)*BLOCK
                col=lax.rem(lax.broadcasted_iota(jnp.int32,(KC,W),1),BLOCK)
                s=jnp.where(key<=col,s,-jnp.inf)
            old=mx[0:1,sl]
            new=jnp.maximum(old,jnp.max(jnp.max(s.reshape(KC//8,8,W),axis=0),axis=0,keepdims=True))
            p=jnp.exp2(s-new)
            dp=lax.dot_general(v,g2[sl,:],NT,preferred_element_type=f32)
            fade=jnp.exp2(old-new)
            sm[:,sl]=sm[:,sl]*fade+jnp.sum(p.reshape(KC//8,8,W),axis=0)
            dl[:,sl]=dl[:,sl]*fade+jnp.sum((p*dp).reshape(KC//8,8,W),axis=0)
            mx[0:1,sl]=new
            mt[i,0:1,sl]=new
            pb[rows,sl]=p.astype(bf)
            dp_s[rows,sl]=dp.astype(dp_s.dtype)
            return 0
        [tile(w,0) for w in range(ROWS//W)]
    def step(i,_):
        forward(i,False)
        return 0
    lax.fori_loop(0,chunks-1,step,0)
    @pl.when(live)
    def _():
        forward(chunks-1,True)
        inv=1.0/jnp.sum(sm[...],axis=0,keepdims=True)
        dl[0:1,:]=jnp.sum(dl[...],axis=0,keepdims=True)*inv
        sm[0:1,:]=inv
    def backward(i,_):
        rows=pl.ds(pl.multiple_of(i*KC,KC),KC)
        kt=kk[rows,:].T
        def tile(w,carry):
            dk,dv=carry
            sl=slice(w*W,(w+1)*W)
            f=sm[0:1,sl]*jnp.exp2(mt[i,0:1,sl]-mx[0:1,sl])
            p=pb[rows,sl].astype(f32)*f
            g=(p*(dp_s[rows,sl].astype(f32)-dl[0:1,sl])).astype(bf)
            dk+=lax.dot_general(g,q2[sl,:],NN,preferred_element_type=f32)
            dv+=lax.dot_general(p.astype(bf),g2[sl,:],NN,preferred_element_type=f32)
            acc[:,sl]+=lax.dot_general(kt,g,NN,preferred_element_type=f32)
            return dk,dv
        zero=jnp.zeros((KC,DH),f32)
        dk,dv=zero,zero
        for w in range(ROWS//W): dk,dv=tile(w,(dk,dv))
        for u in range(NB):
            t=i*NB+u
            b,sz=where_is(t)
            crel=b//4; sx=lax.rem(b,4)
            a=(dk[u*128:(u+1)*128]*scale).astype(bf); e=dv[u*128:(u+1)*128].astype(bf)
            @pl.when((t<n)&(crel==0))
            def _():
                keep_ref[sx,sz,0]=a; keep_ref[sx,sz,1]=e
            @pl.when((t<n)&(crel==1))
            def _():
                send_ref[sx,sz,0]=a; send_ref[sx,sz,1]=e
        return 0
    lax.fori_loop(0,chunks,backward,0)
    for h in range(GROUP):
        sl=slice(h*128,(h+1)*128)
        dq_ref[:,sl]=(acc[:,sl]*scale).T

DPT=f32
def attn_call(me_fn, bounds, q, do, bufs, me=None):
    nb=len(bufs)
    def kern(*refs):
        if me is None: bnd=refs[0]; rest=refs[1:]; mv=me_fn()
        else: mr,bnd=refs[0],refs[1]; rest=refs[2:]; mv=mr[0]
        q_ref,do_ref=rest[:2]; bu=rest[2:2+nb]
        attend_body(mv,bnd,q_ref,do_ref,bu,*rest[2+nb:])
    S=pl.BlockSpec(memory_space=pltpu.SMEM); V=pl.BlockSpec(memory_space=pltpu.VMEM); A=pl.BlockSpec(memory_space=pl.ANY)
    pre=[bounds] if me is None else [me,bounds]
    return pl.pallas_call(kern,
        out_shape=(jax.ShapeDtypeStruct((BLOCK,ROWS),f32),jax.ShapeDtypeStruct((4,4,2,128,128),bf),jax.ShapeDtypeStruct((4,4,2,128,128),bf)),
        in_specs=[S]*len(pre)+[V,V]+[A]*nb, out_specs=(V,V,V),
        scratch_shapes=[pltpu.VMEM((32*BLOCK,DH),bf),pltpu.VMEM((32*BLOCK,DH),bf),pltpu.VMEM((ROWS,DH),bf),pltpu.VMEM((ROWS,DH),bf),
            pltpu.VMEM((32*BLOCK,ROWS),bf),pltpu.VMEM((32*BLOCK,ROWS),DPT),
            pltpu.VMEM((NCH,8,ROWS),f32),
            pltpu.VMEM((8,ROWS),f32),pltpu.VMEM((8,ROWS),f32),pltpu.VMEM((8,ROWS),f32),pltpu.VMEM((DH,ROWS),f32),
            pltpu.SemaphoreType.DMA((2,32))],
        compiler_params=pltpu.CompilerParams(vmem_limit_bytes=48*2**20),
        cost_estimate=pl.CostEstimate(flops=10**10,bytes_accessed=5*2**20,transcendentals=2**22),
    )(*pre,q,do,*bufs)

PAIRS = 8
SLICE_BYTES = 48 * 2**20


def seq_perm(move):
    pairs = []
    for z in range(4):
        for x in range(4):
            for c in range(2):
                nz, nx, nc = move(z, x, c)
                pairs.append(((z * 4 + x) * 2 + c, (nz * 4 + nx) * 2 + nc))
    return pairs


CORE = seq_perm(lambda z, x, c: (z, x, 1 - c))
X_UP = [seq_perm(lambda z, x, c, s=s: (z, (x + s) % 4, c)) for s in range(4)]
X_DOWN = [seq_perm(lambda z, x, c, s=s: (z, (x - s) % 4, c)) for s in range(4)]
X_FLIP = [seq_perm(lambda z, x, c, s=s: (z, x ^ s, c)) for s in (1, 2)]
Z_UP = [seq_perm(lambda z, x, c, s=s: ((z + s) % 4, x, c)) for s in range(4)]
Z_DOWN = [seq_perm(lambda z, x, c, s=s: ((z - s) % 4, x, c)) for s in range(4)]


def head_perm(bit):
    return [(h, h ^ bit) for h in range(8)]


def pack(keys, values, ratios):
    def kern(k_ref, v_ref, ratio_ref, out_ref):
        total = ratio_ref[0]
        for t in range(1, ratios.shape[0]):
            total = total + ratio_ref[t]
        whole = jnp.full((16, DH), total, f32)
        hi = whole.astype(bf).astype(f32)
        mid = (whole - hi).astype(bf).astype(f32)
        low = whole - hi - mid
        row = lax.broadcasted_iota(jnp.int32, (16, DH), 0)
        ride = jnp.where(row == 0, hi, jnp.where(row == 1, mid, jnp.where(row == 2, low, 0.0)))
        out_ref[:BLOCK, :] = k_ref[...]
        out_ref[BLOCK : 2 * BLOCK, :] = v_ref[...]
        out_ref[2 * BLOCK :, :] = ride.astype(bf)

    S = pl.BlockSpec(memory_space=pltpu.SMEM)
    V = pl.BlockSpec(memory_space=pltpu.VMEM)
    return pl.pallas_call(
        kern,
        out_shape=jax.ShapeDtypeStruct((2 * BLOCK + 16, DH), bf),
        in_specs=[V, V, S],
        out_specs=V,
    )(keys, values, ratios)


def unpack(bounds, packets):
    def kern(b_ref, p0, p1, p2, p3, col_ref, sums_ref):
        me = lax.axis_index("seq")
        row = lax.broadcasted_iota(jnp.int32, (RESP, DH), 0)
        sums = jnp.zeros((RESP, DH), f32)
        for s, packet in enumerate((p0, p1, p2, p3)):
            col_ref[s, 0] = packet[:BLOCK, :]
            col_ref[s, 1] = packet[BLOCK : 2 * BLOCK, :]
            first = (lax.rem(me // 8 - s + 4, 4) * 8 + lax.rem(me, 8)) * BLOCK
            resp = jnp.int32(-1)
            for r in range(RESP):
                resp = resp + (first >= b_ref[r]).astype(jnp.int32)
            part = jnp.sum(packet[2 * BLOCK :, :].astype(f32), axis=0, keepdims=True)
            sums = sums + jnp.where(row == resp, part, 0.0)
        sums_ref[...] = sums

    S = pl.BlockSpec(memory_space=pltpu.SMEM)
    V = pl.BlockSpec(memory_space=pltpu.VMEM)
    return pl.pallas_call(
        kern,
        out_shape=(
            jax.ShapeDtypeStruct((4, 2, BLOCK, DH), bf),
            jax.ShapeDtypeStruct((RESP, DH), f32),
        ),
        in_specs=[S, V, V, V, V],
        out_specs=(V, V),
    )(bounds, *packets)


def core_add(sums, bounds, pairs, keep, got):
    def kern(sums_ref, b_ref, p_ref, keep_ref, got_ref, o0, o1, o2, o3, w_ref, mean, coef):
        me = lax.axis_index("seq")
        for r in range(RESP):
            mean[r] = sums_ref[r, 0] / (b_ref[r + 1] - b_ref[r]).astype(f32)
            coef[r] = 0.0
        for p in range(PAIRS):
            win, lose = p_ref[p, 0], p_ref[p, 1]
            resid = mean[win] - mean[lose] - 1.0
            coef[win] = coef[win] + resid
            coef[lose] = coef[lose] - resid

        def weight(block):
            first = block * BLOCK
            w = jnp.float32(0.0)
            for r in range(RESP):
                inside = (first >= b_ref[r]) & (first < b_ref[r + 1])
                length = (b_ref[r + 1] - b_ref[r]).astype(f32)
                w = jnp.where(inside, 512.0 * (2.0 / PAIRS * coef[r] / length), w)
            return w

        mine = weight(me)
        theirs = weight(me + 1 - 2 * lax.rem(me, 2))
        w_ref[...] = jnp.full(w_ref.shape, mine, f32)
        for sx, out in enumerate((o0, o1, o2, o3)):
            for sz in range(4):
                for kvi in range(2):
                    out[sz, kvi] = (
                        keep_ref[sx, sz, kvi].astype(f32) * mine
                        + got_ref[sx, sz, kvi].astype(f32) * theirs
                    ).astype(bf)

    S = pl.BlockSpec(memory_space=pltpu.SMEM)
    V = pl.BlockSpec(memory_space=pltpu.VMEM)
    slot = jax.ShapeDtypeStruct((4, 2, 128, 128), bf)
    return pl.pallas_call(
        kern,
        out_shape=(slot, slot, slot, slot, jax.ShapeDtypeStruct((8, 128), f32)),
        in_specs=[S, S, S, V, V],
        out_specs=(V,) * 5,
        scratch_shapes=[pltpu.SMEM((RESP,), f32), pltpu.SMEM((RESP,), f32)],
        compiler_params=pltpu.CompilerParams(vmem_limit_bytes=SLICE_BYTES),
    )(sums, bounds, pairs, keep, got)


def x_add(a0, a1, a2, a3):
    def kern(i0, i1, i2, i3, *outs):
        for sz in range(4):
            for kvi in range(2):
                outs[sz][kvi] = (
                    (i0[sz, kvi].astype(f32) + i1[sz, kvi].astype(f32))
                    + (i2[sz, kvi].astype(f32) + i3[sz, kvi].astype(f32))
                ).astype(bf)

    V = pl.BlockSpec(memory_space=pltpu.VMEM)
    slot = jax.ShapeDtypeStruct((2, 128, 128), bf)
    return pl.pallas_call(
        kern,
        out_shape=(slot,) * 4,
        in_specs=[V] * 4,
        out_specs=(V,) * 4,
        compiler_params=pltpu.CompilerParams(vmem_limit_bytes=SLICE_BYTES),
    )(a0, a1, a2, a3)


def z_add(a0, a1, a2, a3):
    def kern(i0, i1, i2, i3, dk, dv):
        for kvi, out in enumerate((dk, dv)):
            out[...] = (
                (i0[kvi].astype(f32) + i1[kvi].astype(f32))
                + (i2[kvi].astype(f32) + i3[kvi].astype(f32))
            ).astype(bf)

    V = pl.BlockSpec(memory_space=pltpu.VMEM)
    out = jax.ShapeDtypeStruct((BLOCK, DH), bf)
    return pl.pallas_call(
        kern,
        out_shape=(out, out),
        in_specs=[V] * 4,
        out_specs=(V, V),
    )(a0, a1, a2, a3)


def shards(query_rows, key_rows, value_rows, out_grad, log_ratio, block_mask, bounds, pairs):
    def seq(v, perm):
        return lax.ppermute(v, "seq", perm)

    packet = pack(key_rows, value_rows, log_ratio)
    by_z = [packet] + [seq(packet, Z_UP[s]) for s in (1, 2, 3)]
    column, sums = unpack(bounds, by_z)
    by_x = [column] + [seq(column, X_UP[s]) for s in (1, 2, 3)]
    own_other = seq(column, CORE)
    for bit in (1, 2, 4):
        sums = sums + lax.ppermute(sums, "heads", head_perm(bit))
    sums, by_x, own_other = lax.optimization_barrier((sums, by_x, own_other))
    bufs = by_x + [own_other] + [seq(b, CORE) for b in by_x[1:]]
    sums = sums + seq(sums, CORE)
    sums = sums + seq(sums, X_FLIP[0])
    sums, bufs = lax.optimization_barrier((sums, bufs))
    dq, keep, send = attn_call(lambda: lax.axis_index("seq"), bounds, query_rows, out_grad, bufs)
    sums = sums + seq(sums, X_FLIP[1])
    got = seq(send, CORE)
    *by_shift, weight = core_add(sums, bounds, pairs, keep, got)
    summed = x_add(by_shift[0], *[seq(by_shift[s], X_DOWN[s]) for s in (1, 2, 3)])
    query_grad = (dq * weight[0, 0]).astype(bf)
    key_grad, value_grad = z_add(summed[0], *[seq(summed[s], Z_DOWN[s]) for s in (1, 2, 3)])
    return query_grad, key_grad, value_grad


def solution(mesh):
    whole = P("seq", "heads")
    return jax.shard_map(
        shards,
        mesh=mesh,
        in_specs=(whole, whole, whole, whole, P(("seq", "heads")), P(), P(), P()),
        out_specs=(whole, whole, whole),
        check_vma=False,
    )
```

```python
import math

import jax
import jax.numpy as jnp
from jax import lax
from jax.experimental import pallas as pl
from jax.experimental.pallas import tpu as pltpu
from jax.sharding import PartitionSpec as P

DH = 128
BLOCK = 128
RESP = 8
GROUP = 8
ROWS = GROUP * BLOCK
PACKET = 2 * BLOCK + 16
NB = 4
KC = NB * BLOCK
scale = 1.0 / math.sqrt(DH)
c2 = scale * math.log2(math.e)
f32 = jnp.float32
bf = jnp.bfloat16
NT = (((1,), (1,)), ((), ()))
NN = (((1,), (0,)), ((), ()))
S = pl.BlockSpec(memory_space=pltpu.SMEM)
V = pl.BlockSpec(memory_space=pltpu.VMEM)
A = pl.BlockSpec(memory_space=pl.ANY)


def attend_body(
    bounds, q_ref, do_ref, bufs, dq_ref, keep_ref, send_ref,
    kk, vv, q2, g2, pb, dp_s, mt, mx, sm, dl, acc, sem,
):
    me = lax.axis_index("seq")
    prompt = bounds[0] // BLOCK
    start = jnp.int32(0)
    for r in range(RESP):
        lo = bounds[r] // BLOCK
        start = jnp.where(me >= lo, lo, start)
    live = me >= prompt
    n = jnp.where(live, prompt + me - start + 1, 0)
    chunks = (n + NB - 1) // NB
    z = me // 8
    x = lax.rem(me // 2, 4)
    c = lax.rem(me, 2)

    def where_is(t):
        j = jnp.where(t < prompt, t, start + t - prompt)
        column = lax.rem(lax.rem(j, 2) + c, 2) * 4 + lax.rem(x - lax.rem(j // 2, 4) + 4, 4)
        return column, lax.rem(z - j // 8 + 4, 4)

    def rows_of(t):
        return pl.ds(pl.multiple_of(t * BLOCK, BLOCK), BLOCK)

    def fetch(t, _):
        b, sz = where_is(t)
        for nb, buf in enumerate(bufs):

            @pl.when(b == nb)
            def _(buf=buf):
                key, value = buf.at[sz, pl.ds(0, BLOCK)], buf.at[sz, pl.ds(BLOCK, BLOCK)]
                pltpu.make_async_copy(key, kk.at[rows_of(t)], sem.at[0, t]).start()
                pltpu.make_async_copy(value, vv.at[rows_of(t)], sem.at[1, t]).start()

        return 0

    lax.fori_loop(0, n, fetch, 0)
    for h in range(GROUP):
        at = slice(h * DH, (h + 1) * DH)
        q2[h * BLOCK : (h + 1) * BLOCK, :] = q_ref[:, at]
        g2[h * BLOCK : (h + 1) * BLOCK, :] = do_ref[:, at]
    keep_ref[...] = jnp.zeros_like(keep_ref)
    send_ref[...] = jnp.zeros_like(send_ref)
    mx[...] = jnp.full_like(mx, -1e30)
    sm[...] = jnp.zeros_like(sm)
    dl[...] = jnp.zeros_like(dl)
    acc[...] = jnp.zeros_like(acc)

    def pad(t, _):
        kk[rows_of(t), :] = jnp.zeros((BLOCK, DH), bf)
        vv[rows_of(t), :] = jnp.zeros((BLOCK, DH), bf)
        return 0

    lax.fori_loop(n, chunks * NB, pad, 0)

    def land(t, _):
        pltpu.make_async_copy(bufs[0].at[0, pl.ds(0, BLOCK)], kk.at[rows_of(t)], sem.at[0, t]).wait()
        pltpu.make_async_copy(bufs[0].at[0, pl.ds(0, BLOCK)], vv.at[rows_of(t)], sem.at[1, t]).wait()
        return 0

    def forward(i, masked):
        rows = pl.ds(pl.multiple_of(i * KC, KC), KC)
        lax.fori_loop(i * NB, jnp.minimum(i * NB + NB, n), land, 0)
        s = lax.dot_general(kk[rows, :], q2[...], NT, preferred_element_type=f32) * c2
        if masked:
            key = lax.broadcasted_iota(jnp.int32, (KC, ROWS), 0) + i * KC - (n - 1) * BLOCK
            query = lax.rem(lax.broadcasted_iota(jnp.int32, (KC, ROWS), 1), BLOCK)
            s = jnp.where(key <= query, s, -jnp.inf)
        old = mx[0:1, :]
        top = jnp.max(s.reshape(KC // 8, 8, ROWS), axis=0)
        new = jnp.maximum(old, jnp.max(top, axis=0, keepdims=True))
        p = jnp.exp2(s - new)
        dp = lax.dot_general(vv[rows, :], g2[...], NT, preferred_element_type=f32)
        fade = jnp.exp2(old - new)
        sm[...] = sm[...] * fade + jnp.sum(p.reshape(KC // 8, 8, ROWS), axis=0)
        dl[...] = dl[...] * fade + jnp.sum((p * dp).reshape(KC // 8, 8, ROWS), axis=0)
        mx[0:1, :] = new
        mt[i, 0:1, :] = new
        pb[rows, :] = p.astype(bf)
        dp_s[rows, :] = dp

    def step(i, _):
        forward(i, False)
        return 0

    lax.fori_loop(0, chunks - 1, step, 0)

    @pl.when(live)
    def _():
        forward(chunks - 1, True)
        inv = 1.0 / jnp.sum(sm[...], axis=0, keepdims=True)
        dl[0:1, :] = jnp.sum(dl[...], axis=0, keepdims=True) * inv
        sm[0:1, :] = inv

    def backward(i, _):
        rows = pl.ds(pl.multiple_of(i * KC, KC), KC)
        f = sm[0:1, :] * jnp.exp2(mt[i, 0:1, :] - mx[0:1, :])
        p = pb[rows, :].astype(f32) * f
        g = (p * (dp_s[rows, :] - dl[0:1, :])).astype(bf)
        dk = lax.dot_general(g, q2[...], NN, preferred_element_type=f32)
        dv = lax.dot_general(p.astype(bf), g2[...], NN, preferred_element_type=f32)
        acc[...] += lax.dot_general(kk[rows, :].T, g, NN, preferred_element_type=f32)
        for u in range(NB):
            t = i * NB + u
            b, sz = where_is(t)
            sx = lax.rem(b, 4)
            dk_u = (dk[u * BLOCK : (u + 1) * BLOCK] * scale).astype(bf)
            dv_u = dv[u * BLOCK : (u + 1) * BLOCK].astype(bf)
            for crel, out in enumerate((keep_ref, send_ref)):

                @pl.when((t < n) & (b // 4 == crel))
                def _(out=out):
                    out[sx, sz, 0] = dk_u
                    out[sx, sz, 1] = dv_u

        return 0

    lax.fori_loop(0, chunks, backward, 0)
    for h in range(GROUP):
        at = slice(h * BLOCK, (h + 1) * BLOCK)
        dq_ref[:, at] = (acc[:, at] * scale).T


def attend(bounds, q, do, bufs):
    nb = len(bufs)

    def kern(*refs):
        attend_body(refs[0], refs[1], refs[2], refs[3 : 3 + nb], *refs[3 + nb :])

    partial = jax.ShapeDtypeStruct((4, 4, 2, BLOCK, DH), bf)
    return pl.pallas_call(
        kern,
        out_shape=(jax.ShapeDtypeStruct((BLOCK, ROWS), f32), partial, partial),
        in_specs=[S, V, V] + [A] * nb,
        out_specs=(V, V, V),
        scratch_shapes=[
            pltpu.VMEM((32 * BLOCK, DH), bf),
            pltpu.VMEM((32 * BLOCK, DH), bf),
            pltpu.VMEM((ROWS, DH), bf),
            pltpu.VMEM((ROWS, DH), bf),
            pltpu.VMEM((32 * BLOCK, ROWS), bf),
            pltpu.VMEM((32 * BLOCK, ROWS), f32),
            pltpu.VMEM((32 // NB, 8, ROWS), f32),
            pltpu.VMEM((8, ROWS), f32),
            pltpu.VMEM((8, ROWS), f32),
            pltpu.VMEM((8, ROWS), f32),
            pltpu.VMEM((DH, ROWS), f32),
            pltpu.SemaphoreType.DMA((2, 32)),
        ],
        compiler_params=pltpu.CompilerParams(vmem_limit_bytes=44 * 2**20),
        cost_estimate=pl.CostEstimate(
            flops=10**10, bytes_accessed=5 * 2**20, transcendentals=2**22
        ),
    )(bounds, q, do, *bufs)

PAIRS = 8
SMALL = pltpu.CompilerParams(vmem_limit_bytes=8 * 2**20)


def seq_perm(move):
    pairs = []
    for z in range(4):
        for x in range(4):
            for c in range(2):
                nz, nx, nc = move(z, x, c)
                pairs.append(((z * 4 + x) * 2 + c, (nz * 4 + nx) * 2 + nc))
    return pairs


CORE = seq_perm(lambda z, x, c: (z, x, 1 - c))
X_UP = [seq_perm(lambda z, x, c, s=s: (z, (x + s) % 4, c)) for s in range(4)]
X_DOWN = [seq_perm(lambda z, x, c, s=s: (z, (x - s) % 4, c)) for s in range(4)]
Z_UP = [seq_perm(lambda z, x, c, s=s: ((z + s) % 4, x, c)) for s in range(4)]
Z_DOWN = [seq_perm(lambda z, x, c, s=s: ((z - s) % 4, x, c)) for s in range(4)]


HEAD_Y = [[(h, h // 4 * 4 + m[h % 4]) for h in range(8)] for m in ((1, 0, 3, 2), (3, 2, 1, 0))]
X_FLIP = [seq_perm(lambda z, x, c, m=m: (z, m[x], c)) for m in ((1, 0, 3, 2), (3, 2, 1, 0))]
HALVES = []
for seq_at in range(32):
    for head_at in range(8):
        far = (head_at // 4 * 4 + seq_at // 8) ^ 6
        HALVES.append(
            (seq_at * 8 + head_at, (far % 4 * 8 + seq_at % 8) * 8 + far // 4 * 4 + head_at % 4)
        )


def pack(keys, values, ratios):
    def kern(k_ref, v_ref, ratio_ref, out_ref):
        total = ratio_ref[0]
        for t in range(1, ratios.shape[0]):
            total = total + ratio_ref[t]
        whole = jnp.full((16, DH), total, f32)
        hi = whole.astype(bf).astype(f32)
        mid = (whole - hi).astype(bf).astype(f32)
        low = whole - hi - mid
        row = lax.broadcasted_iota(jnp.int32, (16, DH), 0)
        ride = jnp.where(row == 0, hi, jnp.where(row == 1, mid, jnp.where(row == 2, low, 0.0)))
        out_ref[:BLOCK, :] = k_ref[...]
        out_ref[BLOCK : 2 * BLOCK, :] = v_ref[...]
        out_ref[2 * BLOCK :, :] = ride.astype(bf)

    return pl.pallas_call(
        kern,
        out_shape=jax.ShapeDtypeStruct((2 * BLOCK + 16, DH), bf),
        in_specs=[V, V, S],
        out_specs=V,
    )(keys, values, ratios)


def block_sums(bounds, packets):
    def kern(b_ref, p0, p1, p2, p3, sums_ref):
        me = lax.axis_index("seq")
        row = lax.broadcasted_iota(jnp.int32, (RESP, DH), 0)
        sums = jnp.zeros((RESP, DH), f32)
        for s, packet in enumerate((p0, p1, p2, p3)):
            first = (lax.rem(me // 8 - s + 4, 4) * 8 + lax.rem(me, 8)) * BLOCK
            resp = jnp.int32(-1)
            for r in range(RESP):
                resp = resp + (first >= b_ref[r]).astype(jnp.int32)
            part = jnp.sum(packet[2 * BLOCK :, :].astype(f32), axis=0, keepdims=True)
            sums = sums + jnp.where(row == resp, part, 0.0)
        sums_ref[...] = sums

    return pl.pallas_call(
        kern,
        out_shape=jax.ShapeDtypeStruct((RESP, DH), f32),
        in_specs=[S, V, V, V, V],
        out_specs=V,
        compiler_params=SMALL,
    )(bounds, *packets)


def core_add(sums, bounds, pairs, keep, got):
    def kern(sums_ref, b_ref, p_ref, keep_ref, got_ref, o0, o1, o2, o3, w_ref, mean, coef):
        me = lax.axis_index("seq")
        for r in range(RESP):
            mean[r] = sums_ref[r, 0] / (b_ref[r + 1] - b_ref[r]).astype(f32)
            coef[r] = 0.0
        for p in range(PAIRS):
            win, lose = p_ref[p, 0], p_ref[p, 1]
            resid = mean[win] - mean[lose] - 1.0
            coef[win] = coef[win] + resid
            coef[lose] = coef[lose] - resid

        def weight(block):
            first = block * BLOCK
            w = jnp.float32(0.0)
            for r in range(RESP):
                inside = (first >= b_ref[r]) & (first < b_ref[r + 1])
                length = (b_ref[r + 1] - b_ref[r]).astype(f32)
                w = jnp.where(inside, 512.0 * (2.0 / PAIRS * coef[r] / length), w)
            return w

        mine = weight(me)
        theirs = weight(me + 1 - 2 * lax.rem(me, 2))
        w_ref[...] = jnp.full(w_ref.shape, mine, f32)
        for sx, out in enumerate((o0, o1, o2, o3)):
            for sz in range(4):
                for kvi in range(2):
                    out[sz, kvi] = (
                        keep_ref[sx, sz, kvi].astype(f32) * mine
                        + got_ref[sx, sz, kvi].astype(f32) * theirs
                    ).astype(bf)

    slot = jax.ShapeDtypeStruct((4, 2, 128, 128), bf)
    return pl.pallas_call(
        kern,
        out_shape=(slot, slot, slot, slot, jax.ShapeDtypeStruct((8, 128), f32)),
        in_specs=[S, S, S, V, V],
        out_specs=(V,) * 5,
        scratch_shapes=[pltpu.SMEM((RESP,), f32), pltpu.SMEM((RESP,), f32)],
        compiler_params=SMALL,
    )(sums, bounds, pairs, keep, got)


def x_add(a0, a1, a2, a3):
    def kern(i0, i1, i2, i3, *outs):
        for sz in range(4):
            for kvi in range(2):
                outs[sz][kvi] = (
                    (i0[sz, kvi].astype(f32) + i1[sz, kvi].astype(f32))
                    + (i2[sz, kvi].astype(f32) + i3[sz, kvi].astype(f32))
                ).astype(bf)

    slot = jax.ShapeDtypeStruct((2, 128, 128), bf)
    return pl.pallas_call(
        kern,
        out_shape=(slot,) * 4,
        in_specs=[V] * 4,
        out_specs=(V,) * 4,
        compiler_params=SMALL,
    )(a0, a1, a2, a3)


def z_add(a0, a1, a2, a3):
    def kern(i0, i1, i2, i3, dk, dv):
        for kvi, out in enumerate((dk, dv)):
            out[...] = (
                (i0[kvi].astype(f32) + i1[kvi].astype(f32))
                + (i2[kvi].astype(f32) + i3[kvi].astype(f32))
            ).astype(bf)

    out = jax.ShapeDtypeStruct((BLOCK, DH), bf)
    return pl.pallas_call(
        kern,
        out_shape=(out, out),
        in_specs=[V] * 4,
        out_specs=(V, V),
        compiler_params=SMALL,
    )(a0, a1, a2, a3)


def shards(query_rows, key_rows, value_rows, out_grad, log_ratio, block_mask, bounds, pairs):
    def seq(v, perm):
        return lax.ppermute(v, "seq", perm)

    packet = pack(key_rows, value_rows, log_ratio)
    by_z = [packet] + [seq(packet, Z_UP[s]) for s in (1, 2, 3)]
    column = jnp.stack([p[: 2 * BLOCK] for p in by_z])
    column, by_z = lax.optimization_barrier((column, by_z))
    by_x = [column] + [seq(column, X_UP[s]) for s in (1, 2, 3)]
    sums = block_sums(bounds, by_z)
    for turn in HEAD_Y:
        sums = sums + lax.ppermute(sums, "heads", turn)
    sums = sums + lax.ppermute(sums, ("seq", "heads"), HALVES)
    sums, by_x = lax.optimization_barrier((sums, by_x))
    bufs = by_x + [seq(b, CORE) for b in by_x]
    sums = sums + seq(sums, CORE)
    sums, bufs = lax.optimization_barrier((sums, bufs))
    turned = seq(sums, X_FLIP[0])
    dq, keep, send = attend(bounds, query_rows, out_grad, bufs)
    sums, send = lax.optimization_barrier((sums + turned, send))
    got = seq(send, CORE)
    sums = sums + seq(sums, X_FLIP[1])
    *by_shift, weight = core_add(sums, bounds, pairs, keep, got)
    summed = x_add(by_shift[0], *[seq(by_shift[s], X_DOWN[s]) for s in (1, 2, 3)])
    query_grad = (dq * weight[0, 0]).astype(bf)
    key_grad, value_grad = z_add(summed[0], *[seq(summed[s], Z_DOWN[s]) for s in (1, 2, 3)])
    return query_grad, key_grad, value_grad


def solution(mesh):
    whole = P("seq", "heads")
    return jax.shard_map(
        shards,
        mesh=mesh,
        in_specs=(whole, whole, whole, whole, P(("seq", "heads")), P(), P(), P()),
        out_specs=(whole, whole, whole),
        check_vma=False,
    )
```

```python
import math

import jax
import jax.numpy as jnp
from jax import lax
from jax.experimental import pallas as pl
from jax.experimental.pallas import tpu as pltpu
from jax.sharding import PartitionSpec as P

DH = 128
BLOCK = 128
RESP = 8
GROUP = 8
ROWS = GROUP * BLOCK
PACKET = 2 * BLOCK + 16
NB = 4
KC = NB * BLOCK
scale = 1.0 / math.sqrt(DH)
c2 = scale * math.log2(math.e)
f32 = jnp.float32
bf = jnp.bfloat16
NT = (((1,), (1,)), ((), ()))
NN = (((1,), (0,)), ((), ()))
S = pl.BlockSpec(memory_space=pltpu.SMEM)
V = pl.BlockSpec(memory_space=pltpu.VMEM)
A = pl.BlockSpec(memory_space=pl.ANY)


def attend_body(
    bounds, q_ref, do_ref, bufs, dq_ref, keep_ref, send_ref,
    kv, q2, g2, pb, dp_s, mt, mx, sm, dl, acc, sem,
):
    me = lax.axis_index("seq")
    prompt = bounds[0] // BLOCK
    start = jnp.int32(0)
    for r in range(RESP):
        lo = bounds[r] // BLOCK
        start = jnp.where(me >= lo, lo, start)
    live = me >= prompt
    n = jnp.where(live, prompt + me - start + 1, 0)
    chunks = (n + NB - 1) // NB
    z = me // 8
    x = lax.rem(me // 2, 4)
    c = lax.rem(me, 2)

    def where_is(t):
        j = jnp.where(t < prompt, t, start + t - prompt)
        column = lax.rem(lax.rem(j, 2) + c, 2) * 4 + lax.rem(x - lax.rem(j // 2, 4) + 4, 4)
        return column, lax.rem(z - j // 8 + 4, 4)

    for zz in range(4):
        sz = lax.rem(z + 4 - zz, 4)
        for nb, buf in enumerate(bufs):
            j = zz * 8 + lax.rem(x + 4 - nb % 4, 4) * 2 + lax.rem(c + nb // 4, 2)
            t = jnp.where(j < prompt, j, j - start + prompt)

            @pl.when(live & (j <= me) & ((j < prompt) | (j >= start)))
            def _(buf=buf, sz=sz, t=t):
                pltpu.make_async_copy(buf.at[sz], kv.at[t], sem.at[t]).start()

    for h in range(GROUP):
        at = slice(h * DH, (h + 1) * DH)
        q2[h * BLOCK : (h + 1) * BLOCK, :] = q_ref[:, at]
        g2[h * BLOCK : (h + 1) * BLOCK, :] = do_ref[:, at]
    keep_ref[...] = jnp.zeros_like(keep_ref)
    send_ref[...] = jnp.zeros_like(send_ref)
    mx[...] = jnp.full_like(mx, -1e30)
    sm[...] = jnp.zeros_like(sm)
    dl[...] = jnp.zeros_like(dl)
    acc[...] = jnp.zeros_like(acc)

    def pad(t, _):
        kv[t] = jnp.zeros((2 * BLOCK, DH), bf)
        return 0

    lax.fori_loop(n, chunks * NB, pad, 0)

    def land(t, _):
        pltpu.make_async_copy(bufs[0].at[0], kv.at[t], sem.at[t]).wait()
        return 0

    def part_of(i, kvi):
        blocks = kv[pl.ds(i * NB, NB), kvi * BLOCK : (kvi + 1) * BLOCK, :]
        return blocks.reshape(KC, DH)

    def forward(i, masked):
        rows = pl.ds(pl.multiple_of(i * KC, KC), KC)
        lax.fori_loop(i * NB, jnp.minimum(i * NB + NB, n), land, 0)
        s = lax.dot_general(part_of(i, 0), q2[...], NT, preferred_element_type=f32) * c2
        if masked:
            key = lax.broadcasted_iota(jnp.int32, (KC, ROWS), 0) + i * KC - (n - 1) * BLOCK
            query = lax.rem(lax.broadcasted_iota(jnp.int32, (KC, ROWS), 1), BLOCK)
            s = jnp.where(key <= query, s, -jnp.inf)
        old = mx[0:1, :]
        top = jnp.max(s.reshape(KC // 8, 8, ROWS), axis=0)
        new = jnp.maximum(old, jnp.max(top, axis=0, keepdims=True))
        p = jnp.exp2(s - new)
        dp = lax.dot_general(part_of(i, 1), g2[...], NT, preferred_element_type=f32)
        fade = jnp.exp2(old - new)
        sm[...] = sm[...] * fade + jnp.sum(p.reshape(KC // 8, 8, ROWS), axis=0)
        dl[...] = dl[...] * fade + jnp.sum((p * dp).reshape(KC // 8, 8, ROWS), axis=0)
        mx[0:1, :] = new
        mt[i, 0:1, :] = new
        pb[rows, :] = p.astype(bf)
        dp_s[rows, :] = dp

    def step(i, _):
        forward(i, False)
        return 0

    lax.fori_loop(0, chunks - 1, step, 0)

    @pl.when(live)
    def _():
        forward(chunks - 1, True)
        inv = 1.0 / jnp.sum(sm[...], axis=0, keepdims=True)
        dl[0:1, :] = jnp.sum(dl[...], axis=0, keepdims=True) * inv
        sm[0:1, :] = inv

    def backward(i, _):
        rows = pl.ds(pl.multiple_of(i * KC, KC), KC)
        f = sm[0:1, :] * jnp.exp2(mt[i, 0:1, :] - mx[0:1, :])
        p = pb[rows, :].astype(f32) * f
        g = (p * (dp_s[rows, :] - dl[0:1, :])).astype(bf)
        dk = lax.dot_general(g, q2[...], NN, preferred_element_type=f32)
        dv = lax.dot_general(p.astype(bf), g2[...], NN, preferred_element_type=f32)
        acc[...] += lax.dot_general(part_of(i, 0).T, g, NN, preferred_element_type=f32)
        for u in range(NB):
            t = i * NB + u
            b, sz = where_is(t)
            sx = lax.rem(b, 4)
            dk_u = (dk[u * BLOCK : (u + 1) * BLOCK] * scale).astype(bf)
            dv_u = dv[u * BLOCK : (u + 1) * BLOCK].astype(bf)
            for crel, out in enumerate((keep_ref, send_ref)):

                @pl.when((t < n) & (b // 4 == crel))
                def _(out=out):
                    out[sx, sz, 0] = dk_u
                    out[sx, sz, 1] = dv_u

        return 0

    lax.fori_loop(0, chunks, backward, 0)
    for h in range(GROUP):
        at = slice(h * BLOCK, (h + 1) * BLOCK)
        dq_ref[:, at] = (acc[:, at] * scale).T


def attend(bounds, q, do, bufs):
    nb = len(bufs)

    def kern(*refs):
        attend_body(refs[0], refs[1], refs[2], refs[3 : 3 + nb], *refs[3 + nb :])

    partial = jax.ShapeDtypeStruct((4, 4, 2, BLOCK, DH), bf)
    return pl.pallas_call(
        kern,
        out_shape=(jax.ShapeDtypeStruct((BLOCK, ROWS), f32), partial, partial),
        in_specs=[S, V, V] + [A] * nb,
        out_specs=(V, V, V),
        scratch_shapes=[
            pltpu.VMEM((32, 2 * BLOCK, DH), bf),
            pltpu.VMEM((ROWS, DH), bf),
            pltpu.VMEM((ROWS, DH), bf),
            pltpu.VMEM((32 * BLOCK, ROWS), bf),
            pltpu.VMEM((32 * BLOCK, ROWS), f32),
            pltpu.VMEM((32 // NB, 8, ROWS), f32),
            pltpu.VMEM((8, ROWS), f32),
            pltpu.VMEM((8, ROWS), f32),
            pltpu.VMEM((8, ROWS), f32),
            pltpu.VMEM((DH, ROWS), f32),
            pltpu.SemaphoreType.DMA((32,)),
        ],
        compiler_params=pltpu.CompilerParams(vmem_limit_bytes=36 * 2**20),
        cost_estimate=pl.CostEstimate(
            flops=10**10, bytes_accessed=5 * 2**20, transcendentals=2**22
        ),
    )(bounds, q, do, *bufs)

PAIRS = 8
SMALL = pltpu.CompilerParams(vmem_limit_bytes=8 * 2**20)


def seq_perm(move):
    pairs = []
    for z in range(4):
        for x in range(4):
            for c in range(2):
                nz, nx, nc = move(z, x, c)
                pairs.append(((z * 4 + x) * 2 + c, (nz * 4 + nx) * 2 + nc))
    return pairs


CORE = seq_perm(lambda z, x, c: (z, x, 1 - c))
X_UP = [seq_perm(lambda z, x, c, s=s: (z, (x + s) % 4, c)) for s in range(4)]
X_DOWN = [seq_perm(lambda z, x, c, s=s: (z, (x - s) % 4, c)) for s in range(4)]
Z_UP = [seq_perm(lambda z, x, c, s=s: ((z + s) % 4, x, c)) for s in range(4)]
Z_DOWN = [seq_perm(lambda z, x, c, s=s: ((z - s) % 4, x, c)) for s in range(4)]


HEAD_Y = [[(h, h // 4 * 4 + m[h % 4]) for h in range(8)] for m in ((1, 0, 3, 2), (3, 2, 1, 0))]
X_FLIP = [seq_perm(lambda z, x, c, m=m: (z, m[x], c)) for m in ((1, 0, 3, 2), (3, 2, 1, 0))]
HALVES = []
for seq_at in range(32):
    for head_at in range(8):
        far = (head_at // 4 * 4 + seq_at // 8) ^ 6
        HALVES.append(
            (seq_at * 8 + head_at, (far % 4 * 8 + seq_at % 8) * 8 + far // 4 * 4 + head_at % 4)
        )


def pack(keys, values, ratios):
    def kern(k_ref, v_ref, ratio_ref, out_ref):
        total = ratio_ref[0]
        for t in range(1, ratios.shape[0]):
            total = total + ratio_ref[t]
        whole = jnp.full((16, DH), total, f32)
        hi = whole.astype(bf).astype(f32)
        mid = (whole - hi).astype(bf).astype(f32)
        low = whole - hi - mid
        row = lax.broadcasted_iota(jnp.int32, (16, DH), 0)
        ride = jnp.where(row == 0, hi, jnp.where(row == 1, mid, jnp.where(row == 2, low, 0.0)))
        out_ref[:BLOCK, :] = k_ref[...]
        out_ref[BLOCK : 2 * BLOCK, :] = v_ref[...]
        out_ref[2 * BLOCK :, :] = ride.astype(bf)

    return pl.pallas_call(
        kern,
        out_shape=jax.ShapeDtypeStruct((2 * BLOCK + 16, DH), bf),
        in_specs=[V, V, S],
        out_specs=V,
    )(keys, values, ratios)


def block_sums(bounds, packets):
    def kern(b_ref, p0, p1, p2, p3, sums_ref, rides, sem):
        copies = [
            pltpu.make_async_copy(p.at[pl.ds(2 * BLOCK, 16)], rides.at[k], sem.at[k])
            for k, p in enumerate((p0, p1, p2, p3))
        ]
        for copy in copies:
            copy.start()
        me = lax.axis_index("seq")
        row = lax.broadcasted_iota(jnp.int32, (RESP, DH), 0)
        sums = jnp.zeros((RESP, DH), f32)
        for s in range(4):
            first = (lax.rem(me // 8 - s + 4, 4) * 8 + lax.rem(me, 8)) * BLOCK
            resp = jnp.int32(-1)
            for r in range(RESP):
                resp = resp + (first >= b_ref[r]).astype(jnp.int32)
            copies[s].wait()
            part = jnp.sum(rides[s].astype(f32), axis=0, keepdims=True)
            sums = sums + jnp.where(row == resp, part, 0.0)
        sums_ref[...] = sums

    return pl.pallas_call(
        kern,
        out_shape=jax.ShapeDtypeStruct((RESP, DH), f32),
        in_specs=[S, A, A, A, A],
        out_specs=V,
        scratch_shapes=[pltpu.VMEM((4, 16, DH), bf), pltpu.SemaphoreType.DMA((4,))],
        compiler_params=SMALL,
    )(bounds, *packets)


def core_add(sums, bounds, pairs, keep, got):
    def kern(sums_ref, b_ref, p_ref, keep_ref, got_ref, o0, o1, o2, o3, w_ref, mean, coef):
        me = lax.axis_index("seq")
        for r in range(RESP):
            mean[r] = sums_ref[r, 0] / (b_ref[r + 1] - b_ref[r]).astype(f32)
            coef[r] = 0.0
        for p in range(PAIRS):
            win, lose = p_ref[p, 0], p_ref[p, 1]
            resid = mean[win] - mean[lose] - 1.0
            coef[win] = coef[win] + resid
            coef[lose] = coef[lose] - resid

        def weight(block):
            first = block * BLOCK
            w = jnp.float32(0.0)
            for r in range(RESP):
                inside = (first >= b_ref[r]) & (first < b_ref[r + 1])
                length = (b_ref[r + 1] - b_ref[r]).astype(f32)
                w = jnp.where(inside, 512.0 * (2.0 / PAIRS * coef[r] / length), w)
            return w

        mine = weight(me)
        theirs = weight(me + 1 - 2 * lax.rem(me, 2))
        w_ref[...] = jnp.full(w_ref.shape, mine, f32)
        for sx, out in enumerate((o0, o1, o2, o3)):
            for sz in range(4):
                for kvi in range(2):
                    out[sz, kvi] = (
                        keep_ref[sx, sz, kvi].astype(f32) * mine
                        + got_ref[sx, sz, kvi].astype(f32) * theirs
                    ).astype(bf)

    slot = jax.ShapeDtypeStruct((4, 2, 128, 128), bf)
    return pl.pallas_call(
        kern,
        out_shape=(slot, slot, slot, slot, jax.ShapeDtypeStruct((8, 128), f32)),
        in_specs=[S, S, S, V, V],
        out_specs=(V,) * 5,
        scratch_shapes=[pltpu.SMEM((RESP,), f32), pltpu.SMEM((RESP,), f32)],
        compiler_params=SMALL,
    )(sums, bounds, pairs, keep, got)


def x_add(a0, a1, a2, a3):
    def kern(i0, i1, i2, i3, *outs):
        for sz in range(4):
            for kvi in range(2):
                outs[sz][kvi] = (
                    (i0[sz, kvi].astype(f32) + i1[sz, kvi].astype(f32))
                    + (i2[sz, kvi].astype(f32) + i3[sz, kvi].astype(f32))
                ).astype(bf)

    slot = jax.ShapeDtypeStruct((2, 128, 128), bf)
    return pl.pallas_call(
        kern,
        out_shape=(slot,) * 4,
        in_specs=[V] * 4,
        out_specs=(V,) * 4,
        compiler_params=SMALL,
    )(a0, a1, a2, a3)


def z_add(a0, a1, a2, a3):
    def kern(i0, i1, i2, i3, dk, dv):
        for kvi, out in enumerate((dk, dv)):
            out[...] = (
                (i0[kvi].astype(f32) + i1[kvi].astype(f32))
                + (i2[kvi].astype(f32) + i3[kvi].astype(f32))
            ).astype(bf)

    out = jax.ShapeDtypeStruct((BLOCK, DH), bf)
    return pl.pallas_call(
        kern,
        out_shape=(out, out),
        in_specs=[V] * 4,
        out_specs=(V, V),
        compiler_params=SMALL,
    )(a0, a1, a2, a3)


def shards(query_rows, key_rows, value_rows, out_grad, log_ratio, block_mask, bounds, pairs):
    def seq(v, perm):
        return lax.ppermute(v, "seq", perm)

    packet = pack(key_rows, value_rows, log_ratio)
    by_z = [packet] + [seq(packet, Z_UP[s]) for s in (1, 2, 3)]
    column = jnp.stack([p[: 2 * BLOCK] for p in by_z])
    column, by_z = lax.optimization_barrier((column, by_z))
    far = seq(column, X_UP[2])
    sums, column = lax.optimization_barrier((block_sums(bounds, by_z), column))
    turned = lax.ppermute(sums, "heads", HEAD_Y[0])
    before = seq(column, X_UP[1])
    sums, column = lax.optimization_barrier((sums + turned, column))
    turned = lax.ppermute(sums, "heads", HEAD_Y[1])
    after = seq(column, X_UP[3])
    sums = sums + turned
    by_x = [column, before, far, after]
    sums = sums + lax.ppermute(sums, ("seq", "heads"), HALVES)
    sums, by_x = lax.optimization_barrier((sums, by_x))
    bufs = by_x + [seq(b, CORE) for b in by_x]
    sums = sums + seq(sums, CORE)
    sums, bufs = lax.optimization_barrier((sums, bufs))
    turned = seq(sums, X_FLIP[0])
    dq, keep, send = attend(bounds, query_rows, out_grad, bufs)
    sums, send = lax.optimization_barrier((sums + turned, send))
    got = seq(send, CORE)
    sums = sums + seq(sums, X_FLIP[1])
    *by_shift, weight = core_add(sums, bounds, pairs, keep, got)
    summed = x_add(by_shift[0], *[seq(by_shift[s], X_DOWN[s]) for s in (1, 2, 3)])
    query_grad = (dq * weight[0, 0]).astype(bf)
    key_grad, value_grad = z_add(summed[0], *[seq(summed[s], Z_DOWN[s]) for s in (1, 2, 3)])
    return query_grad, key_grad, value_grad


def solution(mesh):
    whole = P("seq", "heads")
    return jax.shard_map(
        shards,
        mesh=mesh,
        in_specs=(whole, whole, whole, whole, P(("seq", "heads")), P(), P(), P()),
        out_specs=(whole, whole, whole),
        check_vma=False,
    )
```

```python
import math

import jax
import jax.numpy as jnp
from jax import lax
from jax.experimental import pallas as pl
from jax.experimental.pallas import tpu as pltpu
from jax.sharding import PartitionSpec as P

DH = 128
BLOCK = 128
RESP = 8
GROUP = 8
ROWS = GROUP * BLOCK
PACKET = 2 * BLOCK + 16
NB = 4
KC = NB * BLOCK
scale = 1.0 / math.sqrt(DH)
c2 = scale * math.log2(math.e)
f32 = jnp.float32
bf = jnp.bfloat16
NT = (((1,), (1,)), ((), ()))
NN = (((1,), (0,)), ((), ()))
S = pl.BlockSpec(memory_space=pltpu.SMEM)
V = pl.BlockSpec(memory_space=pltpu.VMEM)
A = pl.BlockSpec(memory_space=pl.ANY)


def attend_body(
    bounds, q_ref, do_ref, bufs, dq_ref, keep_ref, send_ref,
    kv, q2, g2, pb, dp_s, mt, mx, sm, dl, acc, sem,
):
    me = lax.axis_index("seq")
    prompt = bounds[0] // BLOCK
    start = jnp.int32(0)
    for r in range(RESP):
        lo = bounds[r] // BLOCK
        start = jnp.where(me >= lo, lo, start)
    live = me >= prompt
    n = jnp.where(live, prompt + me - start + 1, 0)
    chunks = (n + NB - 1) // NB
    z = me // 8
    x = lax.rem(me // 2, 4)
    c = lax.rem(me, 2)

    def where_is(t):
        j = jnp.where(t < prompt, t, start + t - prompt)
        column = lax.rem(lax.rem(j, 2) + c, 2) * 4 + lax.rem(x - lax.rem(j // 2, 4) + 4, 4)
        return column, lax.rem(z - j // 8 + 4, 4)

    for zz in range(4):
        sz = lax.rem(z + 4 - zz, 4)
        for nb, buf in enumerate(bufs):
            j = zz * 8 + lax.rem(x + 4 - nb % 4, 4) * 2 + lax.rem(c + nb // 4, 2)
            t = jnp.where(j < prompt, j, j - start + prompt)

            @pl.when(live & (j <= me) & ((j < prompt) | (j >= start)))
            def _(buf=buf, sz=sz, t=t):
                pltpu.make_async_copy(buf.at[sz], kv.at[t], sem.at[t]).start()

    for h in range(GROUP):
        at = slice(h * DH, (h + 1) * DH)
        q2[h * BLOCK : (h + 1) * BLOCK, :] = q_ref[:, at]
        g2[h * BLOCK : (h + 1) * BLOCK, :] = do_ref[:, at]
    keep_ref[...] = jnp.zeros_like(keep_ref)
    send_ref[...] = jnp.zeros_like(send_ref)
    mx[...] = jnp.full_like(mx, -1e30)
    sm[...] = jnp.zeros_like(sm)
    dl[...] = jnp.zeros_like(dl)
    acc[...] = jnp.zeros_like(acc)

    def pad(t, _):
        kv[t] = jnp.zeros((2 * BLOCK, DH), bf)
        return 0

    lax.fori_loop(n, chunks * NB, pad, 0)

    def land(t, _):
        pltpu.make_async_copy(bufs[0].at[0], kv.at[t], sem.at[t]).wait()
        return 0

    def part_of(i, kvi):
        blocks = kv[pl.ds(i * NB, NB), kvi * BLOCK : (kvi + 1) * BLOCK, :]
        return blocks.reshape(KC, DH)

    def forward(i, masked):
        rows = pl.ds(pl.multiple_of(i * KC, KC), KC)
        lax.fori_loop(i * NB, jnp.minimum(i * NB + NB, n), land, 0)
        s = lax.dot_general(part_of(i, 0), q2[...], NT, preferred_element_type=f32) * c2
        if masked:
            key = lax.broadcasted_iota(jnp.int32, (KC, ROWS), 0) + i * KC - (n - 1) * BLOCK
            query = lax.rem(lax.broadcasted_iota(jnp.int32, (KC, ROWS), 1), BLOCK)
            s = jnp.where(key <= query, s, -jnp.inf)
        old = mx[0:1, :]
        top = jnp.max(s.reshape(KC // 8, 8, ROWS), axis=0)
        new = jnp.maximum(old, jnp.max(top, axis=0, keepdims=True))
        p = jnp.exp2(s - new)
        dp = lax.dot_general(part_of(i, 1), g2[...], NT, preferred_element_type=f32)
        fade = jnp.exp2(old - new)
        sm[...] = sm[...] * fade + jnp.sum(p.reshape(KC // 8, 8, ROWS), axis=0)
        dl[...] = dl[...] * fade + jnp.sum((p * dp).reshape(KC // 8, 8, ROWS), axis=0)
        mx[0:1, :] = new
        mt[i, 0:1, :] = new
        pb[rows, :] = p.astype(bf)
        dp_s[rows, :] = dp

    def step(i, _):
        forward(i, False)
        return 0

    lax.fori_loop(0, chunks - 1, step, 0)

    @pl.when(live)
    def _():
        forward(chunks - 1, True)
        inv = 1.0 / jnp.sum(sm[...], axis=0, keepdims=True)
        dl[0:1, :] = jnp.sum(dl[...], axis=0, keepdims=True) * inv
        sm[0:1, :] = inv

    def backward(i, _):
        rows = pl.ds(pl.multiple_of(i * KC, KC), KC)
        f = sm[0:1, :] * jnp.exp2(mt[i, 0:1, :] - mx[0:1, :])
        p = pb[rows, :].astype(f32) * f
        g = (p * (dp_s[rows, :] - dl[0:1, :])).astype(bf)
        dk = lax.dot_general(g, q2[...], NN, preferred_element_type=f32)
        dv = lax.dot_general(p.astype(bf), g2[...], NN, preferred_element_type=f32)
        acc[...] += lax.dot_general(part_of(i, 0).T, g, NN, preferred_element_type=f32)
        for u in range(NB):
            t = i * NB + u
            b, sz = where_is(t)
            sx = lax.rem(b, 4)
            dk_u = (dk[u * BLOCK : (u + 1) * BLOCK] * scale).astype(bf)
            dv_u = dv[u * BLOCK : (u + 1) * BLOCK].astype(bf)
            for crel, out in enumerate((keep_ref, send_ref)):

                @pl.when((t < n) & (b // 4 == crel))
                def _(out=out):
                    out[sx, sz, 0] = dk_u
                    out[sx, sz, 1] = dv_u

        return 0

    lax.fori_loop(0, chunks, backward, 0)
    for h in range(GROUP):
        at = slice(h * BLOCK, (h + 1) * BLOCK)
        dq_ref[:, at] = (acc[:, at] * scale).T


def attend(bounds, q, do, bufs):
    nb = len(bufs)

    def kern(*refs):
        attend_body(refs[0], refs[1], refs[2], refs[3 : 3 + nb], *refs[3 + nb :])

    partial = jax.ShapeDtypeStruct((4, 4, 2, BLOCK, DH), bf)
    return pl.pallas_call(
        kern,
        out_shape=(jax.ShapeDtypeStruct((BLOCK, ROWS), f32), partial, partial),
        in_specs=[S, V, V] + [A] * nb,
        out_specs=(V, V, V),
        scratch_shapes=[
            pltpu.VMEM((32, 2 * BLOCK, DH), bf),
            pltpu.VMEM((ROWS, DH), bf),
            pltpu.VMEM((ROWS, DH), bf),
            pltpu.VMEM((32 * BLOCK, ROWS), bf),
            pltpu.VMEM((32 * BLOCK, ROWS), f32),
            pltpu.VMEM((32 // NB, 8, ROWS), f32),
            pltpu.VMEM((8, ROWS), f32),
            pltpu.VMEM((8, ROWS), f32),
            pltpu.VMEM((8, ROWS), f32),
            pltpu.VMEM((DH, ROWS), f32),
            pltpu.SemaphoreType.DMA((32,)),
        ],
        compiler_params=pltpu.CompilerParams(vmem_limit_bytes=36 * 2**20),
        cost_estimate=pl.CostEstimate(
            flops=10**10, bytes_accessed=5 * 2**20, transcendentals=2**22
        ),
    )(bounds, q, do, *bufs)

PAIRS = 8
SMALL = pltpu.CompilerParams(vmem_limit_bytes=8 * 2**20)


def seq_perm(move):
    pairs = []
    for z in range(4):
        for x in range(4):
            for c in range(2):
                nz, nx, nc = move(z, x, c)
                pairs.append(((z * 4 + x) * 2 + c, (nz * 4 + nx) * 2 + nc))
    return pairs


CORE = seq_perm(lambda z, x, c: (z, x, 1 - c))
X_UP = [seq_perm(lambda z, x, c, s=s: (z, (x + s) % 4, c)) for s in range(4)]
X_DOWN = [seq_perm(lambda z, x, c, s=s: (z, (x - s) % 4, c)) for s in range(4)]
Z_UP = [seq_perm(lambda z, x, c, s=s: ((z + s) % 4, x, c)) for s in range(4)]
Z_DOWN = [seq_perm(lambda z, x, c, s=s: ((z - s) % 4, x, c)) for s in range(4)]


HEAD_Y = [[(h, h // 4 * 4 + m[h % 4]) for h in range(8)] for m in ((1, 0, 3, 2), (3, 2, 1, 0))]
X_FLIP = [seq_perm(lambda z, x, c, m=m: (z, m[x], c)) for m in ((1, 0, 3, 2), (3, 2, 1, 0))]
HALVES = []
for seq_at in range(32):
    for head_at in range(8):
        far = (head_at // 4 * 4 + seq_at // 8) ^ 6
        HALVES.append(
            (seq_at * 8 + head_at, (far % 4 * 8 + seq_at % 8) * 8 + far // 4 * 4 + head_at % 4)
        )


def pack(keys, values, ratios):
    def kern(k_ref, v_ref, ratio_ref, out_ref):
        total = ratio_ref[0]
        for t in range(1, ratios.shape[0]):
            total = total + ratio_ref[t]
        whole = jnp.full((16, DH), total, f32)
        hi = whole.astype(bf).astype(f32)
        mid = (whole - hi).astype(bf).astype(f32)
        low = whole - hi - mid
        row = lax.broadcasted_iota(jnp.int32, (16, DH), 0)
        ride = jnp.where(row == 0, hi, jnp.where(row == 1, mid, jnp.where(row == 2, low, 0.0)))
        out_ref[:BLOCK, :] = k_ref[...]
        out_ref[BLOCK : 2 * BLOCK, :] = v_ref[...]
        out_ref[2 * BLOCK :, :] = ride.astype(bf)

    return pl.pallas_call(
        kern,
        out_shape=jax.ShapeDtypeStruct((2 * BLOCK + 16, DH), bf),
        in_specs=[V, V, S],
        out_specs=V,
    )(keys, values, ratios)


def block_sums(bounds, ratios, packets):
    def kern(b_ref, ratio_ref, p1, p2, p3, sums_ref, rides, sem):
        copies = [
            pltpu.make_async_copy(p.at[pl.ds(2 * BLOCK, 16)], rides.at[k], sem.at[k])
            for k, p in enumerate((p1, p2, p3))
        ]
        for copy in copies:
            copy.start()
        me = lax.axis_index("seq")
        row = lax.broadcasted_iota(jnp.int32, (RESP, DH), 0)
        own = ratio_ref[0]
        for t in range(1, ratios.shape[0]):
            own = own + ratio_ref[t]
        part = jnp.full((1, DH), own, f32)
        sums = jnp.zeros((RESP, DH), f32)
        for s in range(4):
            first = (lax.rem(me // 8 - s + 4, 4) * 8 + lax.rem(me, 8)) * BLOCK
            resp = jnp.int32(-1)
            for r in range(RESP):
                resp = resp + (first >= b_ref[r]).astype(jnp.int32)
            if s:
                copies[s - 1].wait()
                part = jnp.sum(rides[s - 1].astype(f32), axis=0, keepdims=True)
            sums = sums + jnp.where(row == resp, part, 0.0)
        sums_ref[...] = sums

    return pl.pallas_call(
        kern,
        out_shape=jax.ShapeDtypeStruct((RESP, DH), f32),
        in_specs=[S, S, A, A, A],
        out_specs=V,
        scratch_shapes=[pltpu.VMEM((3, 16, DH), bf), pltpu.SemaphoreType.DMA((3,))],
        compiler_params=SMALL,
    )(bounds, ratios, *packets)


def live_planes(b_ref, z):
    prompt = b_ref[0] // BLOCK
    start = jnp.int32(0)
    for r in range(RESP):
        lo = b_ref[r] // BLOCK
        start = jnp.where(z * 8 >= lo, lo, start)

    def live(plane, column):
        j = plane * 8 + column
        return (plane < z) & ((j < prompt) | ((z * 8 >= prompt) & (j >= start)))

    return live


def slots_needed(bounds):
    def kern(b_ref, out_ref):
        most = jnp.int32(0)
        for z in range(1, 4):
            live = live_planes(b_ref, jnp.int32(z))
            for column in range(8):
                count = jnp.int32(0)
                for plane in range(z):
                    count = count + live(jnp.int32(plane), column).astype(jnp.int32)
                most = jnp.maximum(most, count)
        out_ref[0] = most + 1

    return pl.pallas_call(
        kern,
        out_shape=jax.ShapeDtypeStruct((1,), jnp.int32),
        in_specs=[S],
        out_specs=S,
        compiler_params=SMALL,
    )(bounds)


def core_add(slots, sums, bounds, pairs, keep, got):
    def kern(sums_ref, b_ref, p_ref, keep_ref, got_ref, o0, o1, o2, o3, w_ref, mean, coef):
        me = lax.axis_index("seq")
        for r in range(RESP):
            mean[r] = sums_ref[r, 0] / (b_ref[r + 1] - b_ref[r]).astype(f32)
            coef[r] = 0.0
        for p in range(PAIRS):
            win, lose = p_ref[p, 0], p_ref[p, 1]
            resid = mean[win] - mean[lose] - 1.0
            coef[win] = coef[win] + resid
            coef[lose] = coef[lose] - resid

        def weight(block):
            first = block * BLOCK
            w = jnp.float32(0.0)
            for r in range(RESP):
                inside = (first >= b_ref[r]) & (first < b_ref[r + 1])
                length = (b_ref[r + 1] - b_ref[r]).astype(f32)
                w = jnp.where(inside, 512.0 * (2.0 / PAIRS * coef[r] / length), w)
            return w

        mine = weight(me)
        theirs = weight(me + 1 - 2 * lax.rem(me, 2))
        w_ref[...] = jnp.full(w_ref.shape, mine, f32)
        z = me // 8
        live = live_planes(b_ref, z)
        for sx, out in enumerate((o0, o1, o2, o3)):
            column = lax.rem(me // 2 - sx + 4, 4) * 2 + lax.rem(me, 2)

            def fill(slot, sz, sx=sx, out=out):
                for kvi in range(2):
                    out[slot, kvi] = (
                        keep_ref[sx, sz, kvi].astype(f32) * mine
                        + got_ref[sx, sz, kvi].astype(f32) * theirs
                    ).astype(bf)

            fill(0, 0)
            slot = jnp.int32(1)
            for plane in range(3):
                used = live(jnp.int32(plane), column)

                @pl.when(used)
                def _(slot=slot, plane=plane, fill=fill):
                    fill(slot, z - plane)

                slot = slot + used.astype(jnp.int32)

    slot = jax.ShapeDtypeStruct((slots, 2, 128, 128), bf)
    return pl.pallas_call(
        kern,
        out_shape=(slot, slot, slot, slot, jax.ShapeDtypeStruct((8, 128), f32)),
        in_specs=[S, S, S, V, V],
        out_specs=(V,) * 5,
        scratch_shapes=[pltpu.SMEM((RESP,), f32), pltpu.SMEM((RESP,), f32)],
        compiler_params=SMALL,
    )(sums, bounds, pairs, keep, got)


def x_add(bounds, parts):
    def kern(b_ref, i0, i1, i2, i3, *outs):
        me = lax.axis_index("seq")
        z = me // 8
        live = live_planes(b_ref, z)
        used = [live(jnp.int32(plane), lax.rem(me, 8)).astype(jnp.int32) for plane in range(3)]

        def total(slot, kvi):
            return (
                (i0[slot, kvi].astype(f32) + i1[slot, kvi].astype(f32))
                + (i2[slot, kvi].astype(f32) + i3[slot, kvi].astype(f32))
            ).astype(bf)

        for kvi in range(2):
            outs[0][kvi] = total(0, kvi)
        for sz in range(1, 4):
            plane = z - sz
            slot = 1 + jnp.where(plane > 0, used[0], 0) + jnp.where(plane > 1, used[1], 0)
            here = jnp.int32(0)
            for p in range(3):
                here = jnp.where(plane == p, used[p], here)

            @pl.when(here == 1)
            def _(sz=sz, slot=slot):
                for kvi in range(2):
                    outs[sz][kvi] = total(slot, kvi)

            @pl.when(here == 0)
            def _(sz=sz):
                outs[sz][...] = jnp.zeros_like(outs[sz])

    slot = jax.ShapeDtypeStruct((2, 128, 128), bf)
    return pl.pallas_call(
        kern,
        out_shape=(slot,) * 4,
        in_specs=[S] + [V] * 4,
        out_specs=(V,) * 4,
        compiler_params=SMALL,
    )(bounds, *parts)


def z_add(a0, a1, a2, a3):
    def kern(i0, i1, i2, i3, dk, dv):
        for kvi, out in enumerate((dk, dv)):
            out[...] = (
                (i0[kvi].astype(f32) + i1[kvi].astype(f32))
                + (i2[kvi].astype(f32) + i3[kvi].astype(f32))
            ).astype(bf)

    out = jax.ShapeDtypeStruct((BLOCK, DH), bf)
    return pl.pallas_call(
        kern,
        out_shape=(out, out),
        in_specs=[V] * 4,
        out_specs=(V, V),
        compiler_params=SMALL,
    )(a0, a1, a2, a3)


def shards(query_rows, key_rows, value_rows, out_grad, log_ratio, block_mask, bounds, pairs):
    def seq(v, perm):
        return lax.ppermute(v, "seq", perm)

    packet = pack(key_rows, value_rows, log_ratio)
    slots = slots_needed(bounds)[0]
    by_z = [packet] + [seq(packet, Z_UP[s]) for s in (1, 2, 3)]
    column = jnp.stack([p[: 2 * BLOCK] for p in by_z])
    column, by_z = lax.optimization_barrier((column, by_z))
    far = seq(column, X_UP[2])
    sums, column = lax.optimization_barrier((block_sums(bounds, log_ratio, by_z[1:]), column))
    turned = lax.ppermute(sums, "heads", HEAD_Y[0])
    before = seq(column, X_UP[1])
    sums, column = lax.optimization_barrier((sums + turned, column))
    turned = lax.ppermute(sums, "heads", HEAD_Y[1])
    after = seq(column, X_UP[3])
    sums = sums + turned
    by_x = [column, before, far, after]
    sums = sums + lax.ppermute(sums, ("seq", "heads"), HALVES)
    sums, by_x = lax.optimization_barrier((sums, by_x))
    bufs = by_x + [seq(b, CORE) for b in by_x]
    sums = sums + seq(sums, CORE)
    sums, bufs = lax.optimization_barrier((sums, bufs))
    turned = seq(sums, X_FLIP[0])
    dq, keep, send = attend(bounds, query_rows, out_grad, bufs)
    sums, send = lax.optimization_barrier((sums + turned, send))
    got = seq(send, CORE)
    sums = sums + seq(sums, X_FLIP[1])

    def across_x(slots):
        def branch(sums, keep, got):
            *by_shift, weight = core_add(slots, sums, bounds, pairs, keep, got)
            moved = [seq(by_shift[s], X_DOWN[s]) for s in (1, 2, 3)]
            return x_add(bounds, [by_shift[0]] + moved), weight

        return branch

    summed, weight = lax.switch(
        slots - 2, [across_x(2), across_x(3), across_x(4)], sums, keep, got
    )
    query_grad = (dq * weight[0, 0]).astype(bf)
    key_grad, value_grad = z_add(summed[0], *[seq(summed[s], Z_DOWN[s]) for s in (1, 2, 3)])
    return query_grad, key_grad, value_grad


def solution(mesh):
    whole = P("seq", "heads")
    return jax.shard_map(
        shards,
        mesh=mesh,
        in_specs=(whole, whole, whole, whole, P(("seq", "heads")), P(), P(), P()),
        out_specs=(whole, whole, whole),
        check_vma=False,
    )
```

```python
import math

import jax
import jax.numpy as jnp
from jax import lax
from jax.experimental import pallas as pl
from jax.experimental.pallas import tpu as pltpu
from jax.sharding import PartitionSpec as P

DH = 128
BLOCK = 128
RESP = 8
GROUP = 8
ROWS = GROUP * BLOCK
PACKET = 2 * BLOCK + 16
NB = 4
KC = NB * BLOCK
scale = 1.0 / math.sqrt(DH)
c2 = scale * math.log2(math.e)
f32 = jnp.float32
bf = jnp.bfloat16
NT = (((1,), (1,)), ((), ()))
NN = (((1,), (0,)), ((), ()))
S = pl.BlockSpec(memory_space=pltpu.SMEM)
V = pl.BlockSpec(memory_space=pltpu.VMEM)
A = pl.BlockSpec(memory_space=pl.ANY)


def attend_body(
    bounds, q_ref, do_ref, bufs, dq_ref, keep_ref, send_ref,
    kv, q2, g2, pb, dp_s, mt, mx, sm, dl, acc, sem,
):
    me = lax.axis_index("seq")
    prompt = bounds[0] // BLOCK
    start = jnp.int32(0)
    for r in range(RESP):
        lo = bounds[r] // BLOCK
        start = jnp.where(me >= lo, lo, start)
    live = me >= prompt
    n = jnp.where(live, prompt + me - start + 1, 0)
    chunks = (n + NB - 1) // NB
    z = me // 8
    x = lax.rem(me // 2, 4)
    c = lax.rem(me, 2)

    def where_is(t):
        j = jnp.where(t < prompt, t, start + t - prompt)
        column = lax.rem(lax.rem(j, 2) + c, 2) * 4 + lax.rem(x - lax.rem(j // 2, 4) + 4, 4)
        return column, lax.rem(z - j // 8 + 4, 4)

    for zz in range(4):
        sz = lax.rem(z + 4 - zz, 4)
        for nb, buf in enumerate(bufs):
            j = zz * 8 + lax.rem(x + 4 - nb % 4, 4) * 2 + lax.rem(c + nb // 4, 2)
            t = jnp.where(j < prompt, j, j - start + prompt)

            @pl.when(live & (j <= me) & ((j < prompt) | (j >= start)))
            def _(buf=buf, sz=sz, t=t):
                pltpu.make_async_copy(buf.at[sz], kv.at[t], sem.at[t]).start()

    for h in range(GROUP):
        at = slice(h * DH, (h + 1) * DH)
        q2[h * BLOCK : (h + 1) * BLOCK, :] = q_ref[:, at]
        g2[h * BLOCK : (h + 1) * BLOCK, :] = do_ref[:, at]
    keep_ref[...] = jnp.zeros_like(keep_ref)
    send_ref[...] = jnp.zeros_like(send_ref)
    mx[...] = jnp.full_like(mx, -1e30)
    sm[...] = jnp.zeros_like(sm)
    dl[...] = jnp.zeros_like(dl)
    acc[...] = jnp.zeros_like(acc)

    def pad(t, _):
        kv[t] = jnp.zeros((2 * BLOCK, DH), bf)
        return 0

    lax.fori_loop(n, chunks * NB, pad, 0)

    def land(t, _):
        pltpu.make_async_copy(bufs[0].at[0], kv.at[t], sem.at[t]).wait()
        return 0

    def part_of(i, kvi):
        blocks = kv[pl.ds(i * NB, NB), kvi * BLOCK : (kvi + 1) * BLOCK, :]
        return blocks.reshape(KC, DH)

    def forward(i, masked):
        rows = pl.ds(pl.multiple_of(i * KC, KC), KC)
        lax.fori_loop(i * NB, jnp.minimum(i * NB + NB, n), land, 0)
        s = lax.dot_general(part_of(i, 0), q2[...], NT, preferred_element_type=f32) * c2
        if masked:
            key = lax.broadcasted_iota(jnp.int32, (KC, ROWS), 0) + i * KC - (n - 1) * BLOCK
            query = lax.rem(lax.broadcasted_iota(jnp.int32, (KC, ROWS), 1), BLOCK)
            s = jnp.where(key <= query, s, -jnp.inf)
        old = mx[0:1, :]
        top = jnp.max(s.reshape(KC // 8, 8, ROWS), axis=0)
        new = jnp.maximum(old, jnp.max(top, axis=0, keepdims=True))
        p = jnp.exp2(s - new)
        dp = lax.dot_general(part_of(i, 1), g2[...], NT, preferred_element_type=f32)
        fade = jnp.exp2(old - new)
        sm[...] = sm[...] * fade + jnp.sum(p.reshape(KC // 8, 8, ROWS), axis=0)
        dl[...] = dl[...] * fade + jnp.sum((p * dp).reshape(KC // 8, 8, ROWS), axis=0)
        mx[0:1, :] = new
        mt[i, 0:1, :] = new
        pb[rows, :] = p.astype(bf)
        dp_s[rows, :] = dp

    def step(i, _):
        forward(i, False)
        return 0

    lax.fori_loop(0, chunks - 1, step, 0)

    @pl.when(live)
    def _():
        forward(chunks - 1, True)
        inv = 1.0 / jnp.sum(sm[...], axis=0, keepdims=True)
        dl[0:1, :] = jnp.sum(dl[...], axis=0, keepdims=True) * inv
        sm[0:1, :] = inv

    def backward(i, _):
        rows = pl.ds(pl.multiple_of(i * KC, KC), KC)
        f = sm[0:1, :] * jnp.exp2(mt[i, 0:1, :] - mx[0:1, :])
        p = pb[rows, :].astype(f32) * f
        g = (p * (dp_s[rows, :] - dl[0:1, :])).astype(bf)
        dk = lax.dot_general(g, q2[...], NN, preferred_element_type=f32)
        dv = lax.dot_general(p.astype(bf), g2[...], NN, preferred_element_type=f32)
        acc[...] += lax.dot_general(part_of(i, 0).T, g, NN, preferred_element_type=f32)
        for u in range(NB):
            t = i * NB + u
            b, sz = where_is(t)
            sx = lax.rem(b, 4)
            dk_u = (dk[u * BLOCK : (u + 1) * BLOCK] * scale).astype(bf)
            dv_u = dv[u * BLOCK : (u + 1) * BLOCK].astype(bf)
            for crel, out in enumerate((keep_ref, send_ref)):

                @pl.when((t < n) & (b // 4 == crel))
                def _(out=out):
                    out[sx, sz, 0] = dk_u
                    out[sx, sz, 1] = dv_u

        return 0

    lax.fori_loop(0, chunks, backward, 0)
    for h in range(GROUP):
        at = slice(h * BLOCK, (h + 1) * BLOCK)
        dq_ref[:, at] = (acc[:, at] * scale).T


def attend(bounds, q, do, bufs):
    nb = len(bufs)

    def kern(*refs):
        attend_body(refs[0], refs[1], refs[2], refs[3 : 3 + nb], *refs[3 + nb :])

    partial = jax.ShapeDtypeStruct((4, 4, 2, BLOCK, DH), bf)
    return pl.pallas_call(
        kern,
        out_shape=(jax.ShapeDtypeStruct((BLOCK, ROWS), f32), partial, partial),
        in_specs=[S, V, V] + [A] * nb,
        out_specs=(V, V, V),
        scratch_shapes=[
            pltpu.VMEM((32, 2 * BLOCK, DH), bf),
            pltpu.VMEM((ROWS, DH), bf),
            pltpu.VMEM((ROWS, DH), bf),
            pltpu.VMEM((32 * BLOCK, ROWS), bf),
            pltpu.VMEM((32 * BLOCK, ROWS), f32),
            pltpu.VMEM((32 // NB, 8, ROWS), f32),
            pltpu.VMEM((8, ROWS), f32),
            pltpu.VMEM((8, ROWS), f32),
            pltpu.VMEM((8, ROWS), f32),
            pltpu.VMEM((DH, ROWS), f32),
            pltpu.SemaphoreType.DMA((32,)),
        ],
        compiler_params=pltpu.CompilerParams(vmem_limit_bytes=36 * 2**20),
        cost_estimate=pl.CostEstimate(
            flops=10**10, bytes_accessed=5 * 2**20, transcendentals=2**22
        ),
    )(bounds, q, do, *bufs)

PAIRS = 8
SMALL = pltpu.CompilerParams(vmem_limit_bytes=8 * 2**20)


def seq_perm(move):
    pairs = []
    for z in range(4):
        for x in range(4):
            for c in range(2):
                nz, nx, nc = move(z, x, c)
                pairs.append(((z * 4 + x) * 2 + c, (nz * 4 + nx) * 2 + nc))
    return pairs


CORE = seq_perm(lambda z, x, c: (z, x, 1 - c))
X_UP = [seq_perm(lambda z, x, c, s=s: (z, (x + s) % 4, c)) for s in range(4)]
X_DOWN = [seq_perm(lambda z, x, c, s=s: (z, (x - s) % 4, c)) for s in range(4)]
Z_UP = [seq_perm(lambda z, x, c, s=s: ((z + s) % 4, x, c)) for s in range(4)]
Z_DOWN = [seq_perm(lambda z, x, c, s=s: ((z - s) % 4, x, c)) for s in range(4)]


HEAD_Y = [[(h, h // 4 * 4 + m[h % 4]) for h in range(8)] for m in ((1, 0, 3, 2), (3, 2, 1, 0))]
X_FLIP = [seq_perm(lambda z, x, c, m=m: (z, m[x], c)) for m in ((1, 0, 3, 2), (3, 2, 1, 0))]
HALVES = []
for seq_at in range(32):
    for head_at in range(8):
        far = (head_at // 4 * 4 + seq_at // 8) ^ 6
        HALVES.append(
            (seq_at * 8 + head_at, (far % 4 * 8 + seq_at % 8) * 8 + far // 4 * 4 + head_at % 4)
        )


def pack(keys, values, ratios):
    def kern(k_ref, v_ref, ratio_ref, out_ref):
        total = ratio_ref[0]
        for t in range(1, ratios.shape[0]):
            total = total + ratio_ref[t]
        whole = jnp.full((16, DH), total, f32)
        hi = whole.astype(bf).astype(f32)
        mid = (whole - hi).astype(bf).astype(f32)
        low = whole - hi - mid
        row = lax.broadcasted_iota(jnp.int32, (16, DH), 0)
        ride = jnp.where(row == 0, hi, jnp.where(row == 1, mid, jnp.where(row == 2, low, 0.0)))
        out_ref[:BLOCK, :] = k_ref[...]
        out_ref[BLOCK : 2 * BLOCK, :] = v_ref[...]
        out_ref[2 * BLOCK :, :] = ride.astype(bf)

    return pl.pallas_call(
        kern,
        out_shape=jax.ShapeDtypeStruct((2 * BLOCK + 16, DH), bf),
        in_specs=[V, V, S],
        out_specs=V,
    )(keys, values, ratios)


def block_sums(bounds, total, packets):
    def kern(b_ref, total_ref, p1, p2, p3, sums_ref, rides, sem):
        copies = [
            pltpu.make_async_copy(p.at[pl.ds(2 * BLOCK, 16)], rides.at[k], sem.at[k])
            for k, p in enumerate((p1, p2, p3))
        ]
        for copy in copies:
            copy.start()
        me = lax.axis_index("seq")
        row = lax.broadcasted_iota(jnp.int32, (RESP, DH), 0)
        part = total_ref[...]
        sums = jnp.zeros((RESP, DH), f32)
        for s in range(4):
            first = (lax.rem(me // 8 - s + 4, 4) * 8 + lax.rem(me, 8)) * BLOCK
            resp = jnp.int32(-1)
            for r in range(RESP):
                resp = resp + (first >= b_ref[r]).astype(jnp.int32)
            if s:
                copies[s - 1].wait()
                part = jnp.sum(rides[s - 1].astype(f32), axis=0, keepdims=True)
            sums = sums + jnp.where(row == resp, part, 0.0)
        sums_ref[...] = sums

    return pl.pallas_call(
        kern,
        out_shape=jax.ShapeDtypeStruct((RESP, DH), f32),
        in_specs=[S, V, A, A, A],
        out_specs=V,
        scratch_shapes=[pltpu.VMEM((3, 16, DH), bf), pltpu.SemaphoreType.DMA((3,))],
        compiler_params=SMALL,
    )(bounds, total, *packets)


def live_planes(b_ref, z):
    prompt = b_ref[0] // BLOCK
    start = jnp.int32(0)
    for r in range(RESP):
        lo = b_ref[r] // BLOCK
        start = jnp.where(z * 8 >= lo, lo, start)

    def live(plane, column):
        j = plane * 8 + column
        return (plane < z) & ((j < prompt) | ((z * 8 >= prompt) & (j >= start)))

    return live


def slots_needed(bounds):
    def kern(b_ref, out_ref):
        most = jnp.int32(0)
        for z in range(1, 4):
            live = live_planes(b_ref, jnp.int32(z))
            for column in range(8):
                count = jnp.int32(0)
                for plane in range(z):
                    count = count + live(jnp.int32(plane), column).astype(jnp.int32)
                most = jnp.maximum(most, count)
        out_ref[0] = most + 1

    return pl.pallas_call(
        kern,
        out_shape=jax.ShapeDtypeStruct((1,), jnp.int32),
        in_specs=[S],
        out_specs=S,
        compiler_params=SMALL,
    )(bounds)


def core_add(slots, sums, table, keep, got):
    def kern(sums_ref, b_ref, keep_ref, got_ref, o0, o1, o2, o3, w_ref, mean, coef):
        me = lax.axis_index("seq")
        for r in range(RESP):
            mean[r] = sums_ref[r, 0] / (b_ref[r + 1] - b_ref[r]).astype(f32)
            coef[r] = 0.0
        for p in range(PAIRS):
            win, lose = b_ref[RESP + 1 + 2 * p], b_ref[RESP + 2 + 2 * p]
            resid = mean[win] - mean[lose] - 1.0
            coef[win] = coef[win] + resid
            coef[lose] = coef[lose] - resid

        def weight(block):
            first = block * BLOCK
            w = jnp.float32(0.0)
            for r in range(RESP):
                inside = (first >= b_ref[r]) & (first < b_ref[r + 1])
                length = (b_ref[r + 1] - b_ref[r]).astype(f32)
                w = jnp.where(inside, 512.0 * (2.0 / PAIRS * coef[r] / length), w)
            return w

        mine = weight(me)
        theirs = weight(me + 1 - 2 * lax.rem(me, 2))
        w_ref[...] = jnp.full(w_ref.shape, mine, f32)
        z = me // 8
        live = live_planes(b_ref, z)
        for sx, out in enumerate((o0, o1, o2, o3)):
            column = lax.rem(me // 2 - sx + 4, 4) * 2 + lax.rem(me, 2)

            def fill(slot, sz, sx=sx, out=out):
                for kvi in range(2):
                    out[slot, kvi] = (
                        keep_ref[sx, sz, kvi].astype(f32) * mine
                        + got_ref[sx, sz, kvi].astype(f32) * theirs
                    ).astype(bf)

            fill(0, 0)
            slot = jnp.int32(1)
            for plane in range(3):
                used = live(jnp.int32(plane), column)

                @pl.when(used)
                def _(slot=slot, plane=plane, fill=fill):
                    fill(slot, z - plane)

                slot = slot + used.astype(jnp.int32)

    slot = jax.ShapeDtypeStruct((slots, 2, 128, 128), bf)
    return pl.pallas_call(
        kern,
        out_shape=(slot, slot, slot, slot, jax.ShapeDtypeStruct((8, 128), f32)),
        in_specs=[S, S, V, V],
        out_specs=(V,) * 5,
        scratch_shapes=[pltpu.SMEM((RESP,), f32), pltpu.SMEM((RESP,), f32)],
        compiler_params=SMALL,
    )(sums, table, keep, got)


def x_add(bounds, parts):
    def kern(b_ref, i0, i1, i2, i3, *outs):
        me = lax.axis_index("seq")
        z = me // 8
        live = live_planes(b_ref, z)
        used = [live(jnp.int32(plane), lax.rem(me, 8)).astype(jnp.int32) for plane in range(3)]

        def total(slot, kvi):
            return (
                (i0[slot, kvi].astype(f32) + i1[slot, kvi].astype(f32))
                + (i2[slot, kvi].astype(f32) + i3[slot, kvi].astype(f32))
            ).astype(bf)

        for kvi in range(2):
            outs[0][kvi] = total(0, kvi)
        for sz in range(1, 4):
            plane = z - sz
            slot = 1 + jnp.where(plane > 0, used[0], 0) + jnp.where(plane > 1, used[1], 0)
            here = jnp.int32(0)
            for p in range(3):
                here = jnp.where(plane == p, used[p], here)

            @pl.when(here == 1)
            def _(sz=sz, slot=slot):
                for kvi in range(2):
                    outs[sz][kvi] = total(slot, kvi)

            @pl.when(here == 0)
            def _(sz=sz):
                outs[sz][...] = jnp.zeros_like(outs[sz])

    slot = jax.ShapeDtypeStruct((2, 128, 128), bf)
    return pl.pallas_call(
        kern,
        out_shape=(slot,) * 4,
        in_specs=[S] + [V] * 4,
        out_specs=(V,) * 4,
        compiler_params=SMALL,
    )(bounds, *parts)


def z_add(a0, a1, a2, a3):
    def kern(i0, i1, i2, i3, dk, dv):
        for kvi, out in enumerate((dk, dv)):
            out[...] = (
                (i0[kvi].astype(f32) + i1[kvi].astype(f32))
                + (i2[kvi].astype(f32) + i3[kvi].astype(f32))
            ).astype(bf)

    out = jax.ShapeDtypeStruct((BLOCK, DH), bf)
    return pl.pallas_call(
        kern,
        out_shape=(out, out),
        in_specs=[V] * 4,
        out_specs=(V, V),
        compiler_params=SMALL,
    )(a0, a1, a2, a3)


def shards(query_rows, key_rows, value_rows, out_grad, log_ratio, block_mask, bounds, pairs):
    def seq(v, perm):
        return lax.ppermute(v, "seq", perm)

    packet = pack(key_rows, value_rows, log_ratio)
    by_z = [packet] + [seq(packet, Z_UP[s]) for s in (1, 2, 3)]
    table = jnp.concatenate([bounds, pairs.reshape(2 * PAIRS)])
    total = jnp.broadcast_to(jnp.sum(log_ratio), (1, DH))
    slots = slots_needed(table)
    by_z, table, total, slots = lax.optimization_barrier((by_z, table, total, slots))
    column = jnp.stack([p[: 2 * BLOCK] for p in by_z])
    column, by_z = lax.optimization_barrier((column, by_z))
    far = seq(column, X_UP[2])
    sums, column = lax.optimization_barrier((block_sums(table, total, by_z[1:]), column))
    turned = lax.ppermute(sums, "heads", HEAD_Y[0])
    before = seq(column, X_UP[1])
    sums, column = lax.optimization_barrier((sums + turned, column))
    turned = lax.ppermute(sums, "heads", HEAD_Y[1])
    after = seq(column, X_UP[3])
    sums = sums + turned
    by_x = [column, before, far, after]
    sums = sums + lax.ppermute(sums, ("seq", "heads"), HALVES)
    sums, by_x = lax.optimization_barrier((sums, by_x))
    bufs = by_x + [seq(b, CORE) for b in by_x]
    sums = sums + seq(sums, CORE)
    sums, bufs = lax.optimization_barrier((sums, bufs))
    turned = seq(sums, X_FLIP[0])
    dq, keep, send = attend(table, query_rows, out_grad, bufs)
    sums, send = lax.optimization_barrier((sums + turned, send))
    got = seq(send, CORE)
    sums = sums + seq(sums, X_FLIP[1])

    def across_x(slots):
        def branch(sums, keep, got):
            *by_shift, weight = core_add(slots, sums, table, keep, got)
            moved = [seq(by_shift[s], X_DOWN[s]) for s in (1, 2, 3)]
            return x_add(table, [by_shift[0]] + moved), weight

        return branch

    summed, weight = lax.switch(
        slots[0] - 2, [across_x(2), across_x(3), across_x(4)], sums, keep, got
    )
    query_grad = (dq * weight[0, 0]).astype(bf)
    key_grad, value_grad = z_add(summed[0], *[seq(summed[s], Z_DOWN[s]) for s in (1, 2, 3)])
    return query_grad, key_grad, value_grad


def solution(mesh):
    whole = P("seq", "heads")
    return jax.shard_map(
        shards,
        mesh=mesh,
        in_specs=(whole, whole, whole, whole, P(("seq", "heads")), P(), P(), P()),
        out_specs=(whole, whole, whole),
        check_vma=False,
    )
```

```python
import math

import jax
import jax.numpy as jnp
from jax import lax
from jax.experimental import pallas as pl
from jax.experimental.pallas import tpu as pltpu
from jax.sharding import PartitionSpec as P

DH = 128
BLOCK = 128
RESP = 8
GROUP = 8
ROWS = GROUP * BLOCK
PACKET = 2 * BLOCK + 16
NB = 4
KC = NB * BLOCK
scale = 1.0 / math.sqrt(DH)
c2 = scale * math.log2(math.e)
f32 = jnp.float32
bf = jnp.bfloat16
NT = (((1,), (1,)), ((), ()))
NN = (((1,), (0,)), ((), ()))
S = pl.BlockSpec(memory_space=pltpu.SMEM)
V = pl.BlockSpec(memory_space=pltpu.VMEM)
A = pl.BlockSpec(memory_space=pl.ANY)


def attend_body(
    bounds, q_ref, do_ref, bufs, dq_ref, keep_ref, send_ref,
    kv, q2, g2, pb, dp_s, mt, mx, sm, dl, acc, sem,
):
    me = lax.axis_index("seq")
    prompt = bounds[0] // BLOCK
    start = jnp.int32(0)
    for r in range(RESP):
        lo = bounds[r] // BLOCK
        start = jnp.where(me >= lo, lo, start)
    live = me >= prompt
    n = jnp.where(live, prompt + me - start + 1, 0)
    chunks = (n + NB - 1) // NB
    z = me // 8
    x = lax.rem(me // 2, 4)
    c = lax.rem(me, 2)

    def where_is(t):
        j = jnp.where(t < prompt, t, start + t - prompt)
        column = lax.rem(lax.rem(j, 2) + c, 2) * 4 + lax.rem(x - lax.rem(j // 2, 4) + 4, 4)
        return column, lax.rem(z - j // 8 + 4, 4)

    for zz in range(4):
        sz = lax.rem(z + 4 - zz, 4)
        for nb, buf in enumerate(bufs):
            j = zz * 8 + lax.rem(x + 4 - nb % 4, 4) * 2 + lax.rem(c + nb // 4, 2)
            t = jnp.where(j < prompt, j, j - start + prompt)

            @pl.when(live & (j <= me) & ((j < prompt) | (j >= start)))
            def _(buf=buf, sz=sz, t=t):
                pltpu.make_async_copy(buf.at[sz], kv.at[t], sem.at[t]).start()

    for h in range(GROUP):
        at = slice(h * DH, (h + 1) * DH)
        q2[h * BLOCK : (h + 1) * BLOCK, :] = q_ref[:, at]
        g2[h * BLOCK : (h + 1) * BLOCK, :] = do_ref[:, at]
    keep_ref[...] = jnp.zeros_like(keep_ref)
    send_ref[...] = jnp.zeros_like(send_ref)
    mx[...] = jnp.full_like(mx, -1e30)
    sm[...] = jnp.zeros_like(sm)
    dl[...] = jnp.zeros_like(dl)
    acc[...] = jnp.zeros_like(acc)

    def pad(t, _):
        kv[t] = jnp.zeros((2 * BLOCK, DH), bf)
        return 0

    lax.fori_loop(n, chunks * NB, pad, 0)

    def land(t, _):
        pltpu.make_async_copy(bufs[0].at[0], kv.at[t], sem.at[t]).wait()
        return 0

    def part_of(i, kvi):
        blocks = kv[pl.ds(i * NB, NB), kvi * BLOCK : (kvi + 1) * BLOCK, :]
        return blocks.reshape(KC, DH)

    def forward(i, masked):
        rows = pl.ds(pl.multiple_of(i * KC, KC), KC)
        lax.fori_loop(i * NB, jnp.minimum(i * NB + NB, n), land, 0)
        s = lax.dot_general(part_of(i, 0), q2[...], NT, preferred_element_type=f32) * c2
        if masked:
            key = lax.broadcasted_iota(jnp.int32, (KC, ROWS), 0) + i * KC - (n - 1) * BLOCK
            query = lax.rem(lax.broadcasted_iota(jnp.int32, (KC, ROWS), 1), BLOCK)
            s = jnp.where(key <= query, s, -jnp.inf)
        old = mx[0:1, :]
        top = jnp.max(s.reshape(KC // 8, 8, ROWS), axis=0)
        new = jnp.maximum(old, jnp.max(top, axis=0, keepdims=True))
        p = jnp.exp2(s - new)
        dp = lax.dot_general(part_of(i, 1), g2[...], NT, preferred_element_type=f32)
        fade = jnp.exp2(old - new)
        sm[...] = sm[...] * fade + jnp.sum(p.reshape(KC // 8, 8, ROWS), axis=0)
        dl[...] = dl[...] * fade + jnp.sum((p * dp).reshape(KC // 8, 8, ROWS), axis=0)
        mx[0:1, :] = new
        mt[i, 0:1, :] = new
        pb[rows, :] = p.astype(bf)
        dp_s[rows, :] = dp

    def step(i, _):
        forward(i, False)
        return 0

    lax.fori_loop(0, chunks - 1, step, 0)

    @pl.when(live)
    def _():
        forward(chunks - 1, True)
        inv = 1.0 / jnp.sum(sm[...], axis=0, keepdims=True)
        dl[0:1, :] = jnp.sum(dl[...], axis=0, keepdims=True) * inv
        sm[0:1, :] = inv

    def backward(i, _):
        rows = pl.ds(pl.multiple_of(i * KC, KC), KC)
        f = sm[0:1, :] * jnp.exp2(mt[i, 0:1, :] - mx[0:1, :])
        p = pb[rows, :].astype(f32) * f
        g = (p * (dp_s[rows, :] - dl[0:1, :])).astype(bf)
        dk = lax.dot_general(g, q2[...], NN, preferred_element_type=f32)
        dv = lax.dot_general(p.astype(bf), g2[...], NN, preferred_element_type=f32)
        acc[...] += lax.dot_general(part_of(i, 0).T, g, NN, preferred_element_type=f32)
        for u in range(NB):
            t = i * NB + u
            b, sz = where_is(t)
            sx = lax.rem(b, 4)
            dk_u = (dk[u * BLOCK : (u + 1) * BLOCK] * scale).astype(bf)
            dv_u = dv[u * BLOCK : (u + 1) * BLOCK].astype(bf)
            for crel, out in enumerate((keep_ref, send_ref)):

                @pl.when((t < n) & (b // 4 == crel))
                def _(out=out):
                    out[sx, sz, 0] = dk_u
                    out[sx, sz, 1] = dv_u

        return 0

    lax.fori_loop(0, chunks, backward, 0)
    for h in range(GROUP):
        at = slice(h * BLOCK, (h + 1) * BLOCK)
        dq_ref[:, at] = (acc[:, at] * scale).T


def attend(bounds, q, do, bufs):
    nb = len(bufs)

    def kern(*refs):
        attend_body(refs[0], refs[1], refs[2], refs[3 : 3 + nb], *refs[3 + nb :])

    partial = jax.ShapeDtypeStruct((4, 4, 2, BLOCK, DH), bf)
    return pl.pallas_call(
        kern,
        out_shape=(jax.ShapeDtypeStruct((BLOCK, ROWS), f32), partial, partial),
        in_specs=[S, V, V] + [A] * nb,
        out_specs=(V, V, V),
        scratch_shapes=[
            pltpu.VMEM((32, 2 * BLOCK, DH), bf),
            pltpu.VMEM((ROWS, DH), bf),
            pltpu.VMEM((ROWS, DH), bf),
            pltpu.VMEM((32 * BLOCK, ROWS), bf),
            pltpu.VMEM((32 * BLOCK, ROWS), f32),
            pltpu.VMEM((32 // NB, 8, ROWS), f32),
            pltpu.VMEM((8, ROWS), f32),
            pltpu.VMEM((8, ROWS), f32),
            pltpu.VMEM((8, ROWS), f32),
            pltpu.VMEM((DH, ROWS), f32),
            pltpu.SemaphoreType.DMA((32,)),
        ],
        compiler_params=pltpu.CompilerParams(vmem_limit_bytes=36 * 2**20),
        cost_estimate=pl.CostEstimate(
            flops=10**10, bytes_accessed=5 * 2**20, transcendentals=2**22
        ),
    )(bounds, q, do, *bufs)

PAIRS = 8
SMALL = pltpu.CompilerParams(vmem_limit_bytes=8 * 2**20)


def seq_perm(move):
    pairs = []
    for z in range(4):
        for x in range(4):
            for c in range(2):
                nz, nx, nc = move(z, x, c)
                pairs.append(((z * 4 + x) * 2 + c, (nz * 4 + nx) * 2 + nc))
    return pairs


CORE = seq_perm(lambda z, x, c: (z, x, 1 - c))
X_UP = [seq_perm(lambda z, x, c, s=s: (z, (x + s) % 4, c)) for s in range(4)]
X_DOWN = [seq_perm(lambda z, x, c, s=s: (z, (x - s) % 4, c)) for s in range(4)]
Z_UP = [seq_perm(lambda z, x, c, s=s: ((z + s) % 4, x, c)) for s in range(4)]
Z_DOWN = [seq_perm(lambda z, x, c, s=s: ((z - s) % 4, x, c)) for s in range(4)]


HEAD_Y = [[(h, h // 4 * 4 + m[h % 4]) for h in range(8)] for m in ((1, 0, 3, 2), (3, 2, 1, 0))]
X_FLIP = [seq_perm(lambda z, x, c, m=m: (z, m[x], c)) for m in ((1, 0, 3, 2), (3, 2, 1, 0))]
HALVES = []
for seq_at in range(32):
    for head_at in range(8):
        far = (head_at // 4 * 4 + seq_at // 8) ^ 6
        HALVES.append(
            (seq_at * 8 + head_at, (far % 4 * 8 + seq_at % 8) * 8 + far // 4 * 4 + head_at % 4)
        )


def pack(keys, values, ratios):
    def kern(k_ref, v_ref, ratio_ref, out_ref):
        total = ratio_ref[0]
        for t in range(1, ratios.shape[0]):
            total = total + ratio_ref[t]
        whole = jnp.full((16, DH), total, f32)
        hi = whole.astype(bf).astype(f32)
        mid = (whole - hi).astype(bf).astype(f32)
        low = whole - hi - mid
        row = lax.broadcasted_iota(jnp.int32, (16, DH), 0)
        ride = jnp.where(row == 0, hi, jnp.where(row == 1, mid, jnp.where(row == 2, low, 0.0)))
        out_ref[:BLOCK, :] = k_ref[...]
        out_ref[BLOCK : 2 * BLOCK, :] = v_ref[...]
        out_ref[2 * BLOCK :, :] = ride.astype(bf)

    return pl.pallas_call(
        kern,
        out_shape=jax.ShapeDtypeStruct((2 * BLOCK + 16, DH), bf),
        in_specs=[V, V, S],
        out_specs=V,
    )(keys, values, ratios)


def block_sums(bounds, total, packets):
    def kern(b_ref, total_ref, p1, p2, p3, sums_ref, rides, sem):
        copies = [
            pltpu.make_async_copy(p.at[pl.ds(2 * BLOCK, 16)], rides.at[k], sem.at[k])
            for k, p in enumerate((p1, p2, p3))
        ]
        for copy in copies:
            copy.start()
        me = lax.axis_index("seq")
        row = lax.broadcasted_iota(jnp.int32, (RESP, DH), 0)
        part = jnp.full((1, DH), total_ref[0], f32)
        sums = jnp.zeros((RESP, DH), f32)
        for s in range(4):
            first = (lax.rem(me // 8 - s + 4, 4) * 8 + lax.rem(me, 8)) * BLOCK
            resp = jnp.int32(-1)
            for r in range(RESP):
                resp = resp + (first >= b_ref[r]).astype(jnp.int32)
            if s:
                copies[s - 1].wait()
                part = jnp.sum(rides[s - 1].astype(f32), axis=0, keepdims=True)
            sums = sums + jnp.where(row == resp, part, 0.0)
        sums_ref[...] = sums

    return pl.pallas_call(
        kern,
        out_shape=jax.ShapeDtypeStruct((RESP, DH), f32),
        in_specs=[S, S, A, A, A],
        out_specs=V,
        scratch_shapes=[pltpu.VMEM((3, 16, DH), bf), pltpu.SemaphoreType.DMA((3,))],
        compiler_params=SMALL,
    )(bounds, total, *packets)


def live_planes(b_ref, z):
    prompt = b_ref[0] // BLOCK
    start = jnp.int32(0)
    for r in range(RESP):
        lo = b_ref[r] // BLOCK
        start = jnp.where(z * 8 >= lo, lo, start)

    def live(plane, column):
        j = plane * 8 + column
        return (plane < z) & ((j < prompt) | ((z * 8 >= prompt) & (j >= start)))

    return live


def slots_needed(bounds):
    def kern(b_ref, out_ref):
        most = jnp.int32(0)
        for z in range(1, 4):
            live = live_planes(b_ref, jnp.int32(z))
            for column in range(8):
                count = jnp.int32(0)
                for plane in range(z):
                    count = count + live(jnp.int32(plane), column).astype(jnp.int32)
                most = jnp.maximum(most, count)
        out_ref[0] = most + 1

    return pl.pallas_call(
        kern,
        out_shape=jax.ShapeDtypeStruct((1,), jnp.int32),
        in_specs=[S],
        out_specs=S,
        compiler_params=SMALL,
    )(bounds)


def core_add(slots, sums, table, keep, got):
    def kern(sums_ref, b_ref, keep_ref, got_ref, o0, o1, o2, o3, w_ref, mean, coef):
        me = lax.axis_index("seq")
        for r in range(RESP):
            mean[r] = sums_ref[r, 0] / (b_ref[r + 1] - b_ref[r]).astype(f32)
            coef[r] = 0.0
        for p in range(PAIRS):
            win, lose = b_ref[RESP + 1 + 2 * p], b_ref[RESP + 2 + 2 * p]
            resid = mean[win] - mean[lose] - 1.0
            coef[win] = coef[win] + resid
            coef[lose] = coef[lose] - resid

        def weight(block):
            first = block * BLOCK
            w = jnp.float32(0.0)
            for r in range(RESP):
                inside = (first >= b_ref[r]) & (first < b_ref[r + 1])
                length = (b_ref[r + 1] - b_ref[r]).astype(f32)
                w = jnp.where(inside, 512.0 * (2.0 / PAIRS * coef[r] / length), w)
            return w

        mine = weight(me)
        theirs = weight(me + 1 - 2 * lax.rem(me, 2))
        w_ref[...] = jnp.full(w_ref.shape, mine, f32)
        z = me // 8
        live = live_planes(b_ref, z)
        for sx, out in enumerate((o0, o1, o2, o3)):
            column = lax.rem(me // 2 - sx + 4, 4) * 2 + lax.rem(me, 2)

            def fill(slot, sz, sx=sx, out=out):
                for kvi in range(2):
                    out[slot, kvi] = (
                        keep_ref[sx, sz, kvi].astype(f32) * mine
                        + got_ref[sx, sz, kvi].astype(f32) * theirs
                    ).astype(bf)

            fill(0, 0)
            slot = jnp.int32(1)
            for plane in range(3):
                used = live(jnp.int32(plane), column)

                @pl.when(used)
                def _(slot=slot, plane=plane, fill=fill):
                    fill(slot, z - plane)

                slot = slot + used.astype(jnp.int32)

    slot = jax.ShapeDtypeStruct((slots, 2, 128, 128), bf)
    return pl.pallas_call(
        kern,
        out_shape=(slot, slot, slot, slot, jax.ShapeDtypeStruct((8, ROWS), f32)),
        in_specs=[S, S, V, V],
        out_specs=(V,) * 5,
        scratch_shapes=[pltpu.SMEM((RESP,), f32), pltpu.SMEM((RESP,), f32)],
        compiler_params=SMALL,
    )(sums, table, keep, got)


def x_add(bounds, parts):
    def kern(b_ref, i0, i1, i2, i3, *outs):
        me = lax.axis_index("seq")
        z = me // 8
        live = live_planes(b_ref, z)
        used = [live(jnp.int32(plane), lax.rem(me, 8)).astype(jnp.int32) for plane in range(3)]

        def total(slot, kvi):
            return (
                (i0[slot, kvi].astype(f32) + i1[slot, kvi].astype(f32))
                + (i2[slot, kvi].astype(f32) + i3[slot, kvi].astype(f32))
            ).astype(bf)

        for kvi in range(2):
            outs[0][kvi] = total(0, kvi)
        for sz in range(1, 4):
            plane = z - sz
            slot = 1 + jnp.where(plane > 0, used[0], 0) + jnp.where(plane > 1, used[1], 0)
            here = jnp.int32(0)
            for p in range(3):
                here = jnp.where(plane == p, used[p], here)

            @pl.when(here == 1)
            def _(sz=sz, slot=slot):
                for kvi in range(2):
                    outs[sz][kvi] = total(slot, kvi)

            @pl.when(here == 0)
            def _(sz=sz):
                outs[sz][...] = jnp.zeros_like(outs[sz])

    slot = jax.ShapeDtypeStruct((2, 128, 128), bf)
    return pl.pallas_call(
        kern,
        out_shape=(slot,) * 4,
        in_specs=[S] + [V] * 4,
        out_specs=(V,) * 4,
        compiler_params=SMALL,
    )(bounds, *parts)


def z_add(a0, a1, a2, a3):
    def kern(i0, i1, i2, i3, dk, dv):
        for kvi, out in enumerate((dk, dv)):
            out[...] = (
                (i0[kvi].astype(f32) + i1[kvi].astype(f32))
                + (i2[kvi].astype(f32) + i3[kvi].astype(f32))
            ).astype(bf)

    out = jax.ShapeDtypeStruct((BLOCK, DH), bf)
    return pl.pallas_call(
        kern,
        out_shape=(out, out),
        in_specs=[V] * 4,
        out_specs=(V, V),
        compiler_params=SMALL,
    )(a0, a1, a2, a3)


def shards(query_rows, key_rows, value_rows, out_grad, log_ratio, block_mask, bounds, pairs):
    def seq(v, perm):
        return lax.ppermute(v, "seq", perm)

    packet = pack(key_rows, value_rows, log_ratio)
    by_z = [packet] + [seq(packet, Z_UP[s]) for s in (1, 2, 3)]
    table = jnp.concatenate([bounds, pairs.reshape(2 * PAIRS)])
    total = jnp.sum(log_ratio).reshape(1)
    slots = slots_needed(table)
    moved, table, total, slots = lax.optimization_barrier((by_z[1:], table, total, slots))
    by_z = [packet] + moved
    column = jnp.stack([p[: 2 * BLOCK] for p in by_z])
    column, moved = lax.optimization_barrier((column, moved))
    far = seq(column, X_UP[2])
    sums, column = lax.optimization_barrier((block_sums(table, total, moved), column))
    turned = lax.ppermute(sums, "heads", HEAD_Y[0])
    before = seq(column, X_UP[1])
    sums, column = lax.optimization_barrier((sums + turned, column))
    turned = lax.ppermute(sums, "heads", HEAD_Y[1])
    after = seq(column, X_UP[3])
    sums = sums + turned
    by_x = [column, before, far, after]
    sums = sums + lax.ppermute(sums, ("seq", "heads"), HALVES)
    sums, by_x = lax.optimization_barrier((sums, by_x))
    bufs = by_x + [seq(b, CORE) for b in by_x]
    sums = sums + seq(sums, CORE)
    sums, bufs = lax.optimization_barrier((sums, bufs))
    turned = seq(sums, X_FLIP[0])
    dq, keep, send = attend(table, query_rows, out_grad, bufs)
    sums, send = lax.optimization_barrier((sums + turned, send))
    got = seq(send, CORE)
    sums = sums + seq(sums, X_FLIP[1])

    def across_x(slots):
        def branch(sums, keep, got):
            *by_shift, weight = core_add(slots, sums, table, keep, got)
            moved = [seq(by_shift[s], X_DOWN[s]) for s in (1, 2, 3)]
            return x_add(table, [by_shift[0]] + moved), weight

        return branch

    summed, weight = lax.switch(
        slots[0] - 2, [across_x(2), across_x(3), across_x(4)], sums, keep, got
    )
    query_grad = (dq * weight[:1]).astype(bf)
    key_grad, value_grad = z_add(summed[0], *[seq(summed[s], Z_DOWN[s]) for s in (1, 2, 3)])
    return query_grad, key_grad, value_grad


def solution(mesh):
    whole = P("seq", "heads")
    return jax.shard_map(
        shards,
        mesh=mesh,
        in_specs=(whole, whole, whole, whole, P(("seq", "heads")), P(), P(), P()),
        out_specs=(whole, whole, whole),
        check_vma=False,
    )
```

```python
import math

import jax
import jax.numpy as jnp
from jax import lax
from jax.experimental import pallas as pl
from jax.experimental.pallas import tpu as pltpu
from jax.sharding import PartitionSpec as P

DH = 128
BLOCK = 128
RESP = 8
GROUP = 8
ROWS = GROUP * BLOCK
PACKET = 2 * BLOCK + 16
NB = 4
KC = NB * BLOCK
scale = 1.0 / math.sqrt(DH)
c2 = scale * math.log2(math.e)
f32 = jnp.float32
bf = jnp.bfloat16
NT = (((1,), (1,)), ((), ()))
NN = (((1,), (0,)), ((), ()))
S = pl.BlockSpec(memory_space=pltpu.SMEM)
V = pl.BlockSpec(memory_space=pltpu.VMEM)
A = pl.BlockSpec(memory_space=pl.ANY)


def attend_body(
    bounds, q_ref, do_ref, bufs, dq_ref, keep_ref, send_ref,
    kv, q2, g2, pb, dp_s, mt, mx, sm, dl, acc, sem,
):
    me = lax.axis_index("seq")
    prompt = bounds[0] // BLOCK
    start = jnp.int32(0)
    for r in range(RESP):
        lo = bounds[r] // BLOCK
        start = jnp.where(me >= lo, lo, start)
    live = me >= prompt
    n = jnp.where(live, prompt + me - start + 1, 0)
    chunks = (n + NB - 1) // NB
    z = me // 8
    x = lax.rem(me // 2, 4)
    c = lax.rem(me, 2)

    def where_is(t):
        j = jnp.where(t < prompt, t, start + t - prompt)
        column = lax.rem(lax.rem(j, 2) + c, 2) * 4 + lax.rem(x - lax.rem(j // 2, 4) + 4, 4)
        return column, lax.rem(z - j // 8 + 4, 4)

    for zz in range(4):
        sz = lax.rem(z + 4 - zz, 4)
        for nb, buf in enumerate(bufs):
            j = zz * 8 + lax.rem(x + 4 - nb % 4, 4) * 2 + lax.rem(c + nb // 4, 2)
            t = jnp.where(j < prompt, j, j - start + prompt)

            @pl.when(live & (j <= me) & ((j < prompt) | (j >= start)))
            def _(buf=buf, sz=sz, t=t):
                pltpu.make_async_copy(buf.at[sz], kv.at[t], sem.at[t]).start()

    for h in range(GROUP):
        at = slice(h * DH, (h + 1) * DH)
        q2[h * BLOCK : (h + 1) * BLOCK, :] = q_ref[:, at]
        g2[h * BLOCK : (h + 1) * BLOCK, :] = do_ref[:, at]
    keep_ref[...] = jnp.zeros_like(keep_ref)
    send_ref[...] = jnp.zeros_like(send_ref)
    mx[...] = jnp.full_like(mx, -1e30)
    sm[...] = jnp.zeros_like(sm)
    dl[...] = jnp.zeros_like(dl)
    acc[...] = jnp.zeros_like(acc)

    def pad(t, _):
        kv[t] = jnp.zeros((2 * BLOCK, DH), bf)
        return 0

    lax.fori_loop(n, chunks * NB, pad, 0)

    def land(t, _):
        pltpu.make_async_copy(bufs[0].at[0], kv.at[t], sem.at[t]).wait()
        return 0

    def part_of(i, kvi):
        blocks = kv[pl.ds(i * NB, NB), kvi * BLOCK : (kvi + 1) * BLOCK, :]
        return blocks.reshape(KC, DH)

    def forward(i, masked):
        rows = pl.ds(pl.multiple_of(i * KC, KC), KC)
        lax.fori_loop(i * NB, jnp.minimum(i * NB + NB, n), land, 0)
        s = lax.dot_general(part_of(i, 0), q2[...], NT, preferred_element_type=f32) * c2
        if masked:
            key = lax.broadcasted_iota(jnp.int32, (KC, ROWS), 0) + i * KC - (n - 1) * BLOCK
            query = lax.rem(lax.broadcasted_iota(jnp.int32, (KC, ROWS), 1), BLOCK)
            s = jnp.where(key <= query, s, -jnp.inf)
        old = mx[0:1, :]
        top = jnp.max(s.reshape(KC // 8, 8, ROWS), axis=0)
        new = jnp.maximum(old, jnp.max(top, axis=0, keepdims=True))
        p = jnp.exp2(s - new)
        dp = lax.dot_general(part_of(i, 1), g2[...], NT, preferred_element_type=f32)
        fade = jnp.exp2(old - new)
        sm[...] = sm[...] * fade + jnp.sum(p.reshape(KC // 8, 8, ROWS), axis=0)
        dl[...] = dl[...] * fade + jnp.sum((p * dp).reshape(KC // 8, 8, ROWS), axis=0)
        mx[0:1, :] = new
        mt[i, 0:1, :] = new
        pb[rows, :] = p.astype(bf)
        dp_s[rows, :] = dp

    def step(i, _):
        forward(i, False)
        return 0

    lax.fori_loop(0, chunks - 1, step, 0)

    @pl.when(live)
    def _():
        forward(chunks - 1, True)
        inv = 1.0 / jnp.sum(sm[...], axis=0, keepdims=True)
        dl[0:1, :] = jnp.sum(dl[...], axis=0, keepdims=True) * inv
        sm[0:1, :] = inv

    def backward(i, _):
        rows = pl.ds(pl.multiple_of(i * KC, KC), KC)
        f = sm[0:1, :] * jnp.exp2(mt[i, 0:1, :] - mx[0:1, :])
        p = pb[rows, :].astype(f32) * f
        g = (p * (dp_s[rows, :] - dl[0:1, :])).astype(bf)
        dk = lax.dot_general(g, q2[...], NN, preferred_element_type=f32)
        dv = lax.dot_general(p.astype(bf), g2[...], NN, preferred_element_type=f32)
        acc[...] += lax.dot_general(part_of(i, 0).T, g, NN, preferred_element_type=f32)
        for u in range(NB):
            t = i * NB + u
            b, sz = where_is(t)
            sx = lax.rem(b, 4)
            dk_u = (dk[u * BLOCK : (u + 1) * BLOCK] * scale).astype(bf)
            dv_u = dv[u * BLOCK : (u + 1) * BLOCK].astype(bf)
            for crel, out in enumerate((keep_ref, send_ref)):

                @pl.when((t < n) & (b // 4 == crel))
                def _(out=out):
                    out[sx, sz, 0] = dk_u
                    out[sx, sz, 1] = dv_u

        return 0

    lax.fori_loop(0, chunks, backward, 0)
    for h in range(GROUP):
        at = slice(h * BLOCK, (h + 1) * BLOCK)
        dq_ref[:, at] = (acc[:, at] * scale).T


def attend(bounds, q, do, bufs):
    nb = len(bufs)

    def kern(*refs):
        attend_body(refs[0], refs[1], refs[2], refs[3 : 3 + nb], *refs[3 + nb :])

    partial = jax.ShapeDtypeStruct((4, 4, 2, BLOCK, DH), bf)
    return pl.pallas_call(
        kern,
        out_shape=(jax.ShapeDtypeStruct((BLOCK, ROWS), f32), partial, partial),
        in_specs=[S, V, V] + [A] * nb,
        out_specs=(V, V, V),
        scratch_shapes=[
            pltpu.VMEM((32, 2 * BLOCK, DH), bf),
            pltpu.VMEM((ROWS, DH), bf),
            pltpu.VMEM((ROWS, DH), bf),
            pltpu.VMEM((32 * BLOCK, ROWS), bf),
            pltpu.VMEM((32 * BLOCK, ROWS), f32),
            pltpu.VMEM((32 // NB, 8, ROWS), f32),
            pltpu.VMEM((8, ROWS), f32),
            pltpu.VMEM((8, ROWS), f32),
            pltpu.VMEM((8, ROWS), f32),
            pltpu.VMEM((DH, ROWS), f32),
            pltpu.SemaphoreType.DMA((32,)),
        ],
        compiler_params=pltpu.CompilerParams(vmem_limit_bytes=36 * 2**20),
        cost_estimate=pl.CostEstimate(
            flops=10**10, bytes_accessed=5 * 2**20, transcendentals=2**22
        ),
    )(bounds, q, do, *bufs)

PAIRS = 8
SMALL = pltpu.CompilerParams(vmem_limit_bytes=8 * 2**20)


def seq_perm(move):
    pairs = []
    for z in range(4):
        for x in range(4):
            for c in range(2):
                nz, nx, nc = move(z, x, c)
                pairs.append(((z * 4 + x) * 2 + c, (nz * 4 + nx) * 2 + nc))
    return pairs


CORE = seq_perm(lambda z, x, c: (z, x, 1 - c))
X_UP = [seq_perm(lambda z, x, c, s=s: (z, (x + s) % 4, c)) for s in range(4)]
X_DOWN = [seq_perm(lambda z, x, c, s=s: (z, (x - s) % 4, c)) for s in range(4)]
Z_UP = [seq_perm(lambda z, x, c, s=s: ((z + s) % 4, x, c)) for s in range(4)]
Z_DOWN = [[(i, i - 8 * s) for i in range(8 * s, 32)] for s in range(4)]


HEAD_Y = [[(h, h // 4 * 4 + m[h % 4]) for h in range(8)] for m in ((1, 0, 3, 2), (3, 2, 1, 0))]
X_FLIP = [seq_perm(lambda z, x, c, m=m: (z, m[x], c)) for m in ((1, 0, 3, 2), (3, 2, 1, 0))]
HALVES = []
for seq_at in range(32):
    for head_at in range(8):
        far = (head_at // 4 * 4 + seq_at // 8) ^ 6
        HALVES.append(
            (seq_at * 8 + head_at, (far % 4 * 8 + seq_at % 8) * 8 + far // 4 * 4 + head_at % 4)
        )


def pack(keys, values, ratios):
    def kern(k_ref, v_ref, ratio_ref, out_ref):
        total = ratio_ref[0]
        for t in range(1, ratios.shape[0]):
            total = total + ratio_ref[t]
        whole = jnp.full((16, DH), total, f32)
        hi = whole.astype(bf).astype(f32)
        mid = (whole - hi).astype(bf).astype(f32)
        low = whole - hi - mid
        row = lax.broadcasted_iota(jnp.int32, (16, DH), 0)
        ride = jnp.where(row == 0, hi, jnp.where(row == 1, mid, jnp.where(row == 2, low, 0.0)))
        out_ref[:BLOCK, :] = k_ref[...]
        out_ref[BLOCK : 2 * BLOCK, :] = v_ref[...]
        out_ref[2 * BLOCK :, :] = ride.astype(bf)

    return pl.pallas_call(
        kern,
        out_shape=jax.ShapeDtypeStruct((2 * BLOCK + 16, DH), bf),
        in_specs=[V, V, S],
        out_specs=V,
    )(keys, values, ratios)


def block_sums(bounds, total, packets):
    def kern(b_ref, total_ref, p1, p2, p3, sums_ref, rides, sem):
        copies = [
            pltpu.make_async_copy(p.at[pl.ds(2 * BLOCK, 16)], rides.at[k], sem.at[k])
            for k, p in enumerate((p1, p2, p3))
        ]
        for copy in copies:
            copy.start()
        me = lax.axis_index("seq")
        row = lax.broadcasted_iota(jnp.int32, (RESP, DH), 0)
        part = total_ref[0:1, :]
        sums = jnp.zeros((RESP, DH), f32)
        for s in range(4):
            first = (lax.rem(me // 8 - s + 4, 4) * 8 + lax.rem(me, 8)) * BLOCK
            resp = jnp.int32(-1)
            for r in range(RESP):
                resp = resp + (first >= b_ref[r]).astype(jnp.int32)
            if s:
                copies[s - 1].wait()
                part = jnp.sum(rides[s - 1].astype(f32), axis=0, keepdims=True)
            sums = sums + jnp.where(row == resp, part, 0.0)
        sums_ref[...] = sums

    return pl.pallas_call(
        kern,
        out_shape=jax.ShapeDtypeStruct((RESP, DH), f32),
        in_specs=[S, V, A, A, A],
        out_specs=V,
        scratch_shapes=[pltpu.VMEM((3, 16, DH), bf), pltpu.SemaphoreType.DMA((3,))],
        compiler_params=SMALL,
    )(bounds, total, *packets)


def live_planes(b_ref, z):
    prompt = b_ref[0] // BLOCK
    start = jnp.int32(0)
    for r in range(RESP):
        lo = b_ref[r] // BLOCK
        start = jnp.where(z * 8 >= lo, lo, start)

    def live(plane, column):
        j = plane * 8 + column
        return (plane < z) & ((j < prompt) | ((z * 8 >= prompt) & (j >= start)))

    return live


def small_things(bounds, ratios):
    def kern(b_ref, ratio_ref, out_ref, total_ref):
        most = jnp.int32(0)
        for z in range(1, 4):
            live = live_planes(b_ref, jnp.int32(z))
            for column in range(8):
                count = jnp.int32(0)
                for plane in range(z):
                    count = count + live(jnp.int32(plane), column).astype(jnp.int32)
                most = jnp.maximum(most, count)
        out_ref[0] = most + 1
        total = ratio_ref[0]
        for t in range(1, ratios.shape[0]):
            total = total + ratio_ref[t]
        total_ref[...] = jnp.full(total_ref.shape, total, f32)

    return pl.pallas_call(
        kern,
        out_shape=(
            jax.ShapeDtypeStruct((1,), jnp.int32),
            jax.ShapeDtypeStruct((8, DH), f32),
        ),
        in_specs=[S, S],
        out_specs=(S, V),
        compiler_params=SMALL,
    )(bounds, ratios)


def core_add(slots, sums, table, keep, got):
    def kern(sums_ref, b_ref, keep_ref, got_ref, o0, o1, o2, o3, w_ref, mean, coef):
        me = lax.axis_index("seq")
        for r in range(RESP):
            mean[r] = sums_ref[r, 0] / (b_ref[r + 1] - b_ref[r]).astype(f32)
            coef[r] = 0.0
        for p in range(PAIRS):
            win, lose = b_ref[RESP + 1 + 2 * p], b_ref[RESP + 2 + 2 * p]
            resid = mean[win] - mean[lose] - 1.0
            coef[win] = coef[win] + resid
            coef[lose] = coef[lose] - resid

        def weight(block):
            first = block * BLOCK
            w = jnp.float32(0.0)
            for r in range(RESP):
                inside = (first >= b_ref[r]) & (first < b_ref[r + 1])
                length = (b_ref[r + 1] - b_ref[r]).astype(f32)
                w = jnp.where(inside, 512.0 * (2.0 / PAIRS * coef[r] / length), w)
            return w

        mine = weight(me)
        theirs = weight(me + 1 - 2 * lax.rem(me, 2))
        w_ref[...] = jnp.full(w_ref.shape, mine, f32)
        z = me // 8
        live = live_planes(b_ref, z)
        for sx, out in enumerate((o0, o1, o2, o3)):
            column = lax.rem(me // 2 - sx + 4, 4) * 2 + lax.rem(me, 2)

            def fill(slot, sz, sx=sx, out=out):
                for kvi in range(2):
                    out[slot, kvi] = (
                        keep_ref[sx, sz, kvi].astype(f32) * mine
                        + got_ref[sx, sz, kvi].astype(f32) * theirs
                    ).astype(bf)

            fill(0, 0)
            slot = jnp.int32(1)
            for plane in range(3):
                used = live(jnp.int32(plane), column)

                @pl.when(used)
                def _(slot=slot, plane=plane, fill=fill):
                    fill(slot, z - plane)

                slot = slot + used.astype(jnp.int32)

    slot = jax.ShapeDtypeStruct((slots, 2, 128, 128), bf)
    return pl.pallas_call(
        kern,
        out_shape=(slot, slot, slot, slot, jax.ShapeDtypeStruct((8, ROWS), f32)),
        in_specs=[S, S, V, V],
        out_specs=(V,) * 5,
        scratch_shapes=[pltpu.SMEM((RESP,), f32), pltpu.SMEM((RESP,), f32)],
        compiler_params=SMALL,
    )(sums, table, keep, got)


def x_add(bounds, parts):
    def kern(b_ref, i0, i1, i2, i3, *outs):
        me = lax.axis_index("seq")
        z = me // 8
        live = live_planes(b_ref, z)
        used = [live(jnp.int32(plane), lax.rem(me, 8)).astype(jnp.int32) for plane in range(3)]

        def total(slot, kvi):
            return (
                (i0[slot, kvi].astype(f32) + i1[slot, kvi].astype(f32))
                + (i2[slot, kvi].astype(f32) + i3[slot, kvi].astype(f32))
            ).astype(bf)

        for kvi in range(2):
            outs[0][kvi] = total(0, kvi)
        for sz in range(1, 4):
            plane = z - sz
            slot = 1 + jnp.where(plane > 0, used[0], 0) + jnp.where(plane > 1, used[1], 0)
            here = jnp.int32(0)
            for p in range(3):
                here = jnp.where(plane == p, used[p], here)

            @pl.when(here == 1)
            def _(sz=sz, slot=slot):
                for kvi in range(2):
                    outs[sz][kvi] = total(slot, kvi)

            @pl.when(here == 0)
            def _(sz=sz):
                outs[sz][...] = jnp.zeros_like(outs[sz])

    slot = jax.ShapeDtypeStruct((2, 128, 128), bf)
    return pl.pallas_call(
        kern,
        out_shape=(slot,) * 4,
        in_specs=[S] + [V] * 4,
        out_specs=(V,) * 4,
        compiler_params=SMALL,
    )(bounds, *parts)


def z_add(a0, a1, a2, a3):
    def kern(i0, i1, i2, i3, dk, dv):
        for kvi, out in enumerate((dk, dv)):
            out[...] = (
                (i0[kvi].astype(f32) + i1[kvi].astype(f32))
                + (i2[kvi].astype(f32) + i3[kvi].astype(f32))
            ).astype(bf)

    out = jax.ShapeDtypeStruct((BLOCK, DH), bf)
    return pl.pallas_call(
        kern,
        out_shape=(out, out),
        in_specs=[V] * 4,
        out_specs=(V, V),
        compiler_params=SMALL,
    )(a0, a1, a2, a3)


def shards(query_rows, key_rows, value_rows, out_grad, log_ratio, block_mask, bounds, pairs):
    def seq(v, perm):
        return lax.ppermute(v, "seq", perm)

    packet = pack(key_rows, value_rows, log_ratio)
    by_z = [packet] + [seq(packet, Z_UP[s]) for s in (1, 2, 3)]
    table = jnp.concatenate([bounds, pairs.reshape(2 * PAIRS)])
    slots, total = small_things(table, log_ratio)
    moved, table, total, slots = lax.optimization_barrier((by_z[1:], table, total, slots))
    by_z = [packet] + moved
    column = jnp.stack([p[: 2 * BLOCK] for p in by_z])
    column, moved = lax.optimization_barrier((column, moved))
    far = seq(column, X_UP[2])
    sums, column = lax.optimization_barrier((block_sums(table, total, moved), column))
    turned = lax.ppermute(sums, "heads", HEAD_Y[0])
    before = seq(column, X_UP[1])
    sums, column = lax.optimization_barrier((sums + turned, column))
    turned = lax.ppermute(sums, "heads", HEAD_Y[1])
    after = seq(column, X_UP[3])
    sums = sums + turned
    by_x = [column, before, far, after]
    sums = sums + lax.ppermute(sums, ("seq", "heads"), HALVES)
    sums, by_x = lax.optimization_barrier((sums, by_x))
    bufs = by_x + [seq(b, CORE) for b in by_x]
    sums = sums + seq(sums, CORE)
    sums, bufs = lax.optimization_barrier((sums, bufs))
    turned = seq(sums, X_FLIP[0])
    dq, keep, send = attend(table, query_rows, out_grad, bufs)
    sums, send = lax.optimization_barrier((sums + turned, send))
    got = seq(send, CORE)
    sums = sums + seq(sums, X_FLIP[1])

    def across_x(slots):
        def branch(sums, keep, got):
            *by_shift, weight = core_add(slots, sums, table, keep, got)
            far = seq(by_shift[2], X_DOWN[2])
            near = [seq(by_shift[s], X_DOWN[s]) for s in (1, 3)]
            return x_add(table, [by_shift[0], far] + near), weight

        return branch

    summed, weight = lax.switch(
        slots[0] - 2, [across_x(2), across_x(3), across_x(4)], sums, keep, got
    )
    query_grad = (dq * weight[:1]).astype(bf)
    key_grad, value_grad = z_add(summed[0], *[seq(summed[s], Z_DOWN[s]) for s in (3, 2, 1)])
    return query_grad, key_grad, value_grad


def solution(mesh):
    whole = P("seq", "heads")
    return jax.shard_map(
        shards,
        mesh=mesh,
        in_specs=(whole, whole, whole, whole, P(("seq", "heads")), P(), P(), P()),
        out_specs=(whole, whole, whole),
        check_vma=False,
    )
```

```python
import math

import jax
import jax.numpy as jnp
from jax import lax
from jax.experimental import pallas as pl
from jax.experimental.pallas import tpu as pltpu
from jax.sharding import PartitionSpec as P

DH = 128
BLOCK = 128
RESP = 8
GROUP = 8
ROWS = GROUP * BLOCK
PACKET = 2 * BLOCK + 16
NB = 4
KC = NB * BLOCK
scale = 1.0 / math.sqrt(DH)
c2 = scale * math.log2(math.e)
f32 = jnp.float32
bf = jnp.bfloat16
NT = (((1,), (1,)), ((), ()))
NN = (((1,), (0,)), ((), ()))
S = pl.BlockSpec(memory_space=pltpu.SMEM)
V = pl.BlockSpec(memory_space=pltpu.VMEM)
A = pl.BlockSpec(memory_space=pl.ANY)


def attend_body(
    bounds, q_ref, do_ref, bufs, dq_ref, keep_ref, send_ref,
    kv, q2, g2, pb, dp_s, mt, mx, sm, dl, acc, sem,
):
    me = lax.axis_index("seq")
    prompt = bounds[0] // BLOCK
    start = jnp.int32(0)
    for r in range(RESP):
        lo = bounds[r] // BLOCK
        start = jnp.where(me >= lo, lo, start)
    live = me >= prompt
    n = jnp.where(live, prompt + me - start + 1, 0)
    full = jnp.maximum(n - 1, 0) // NB
    short = n - full * NB <= NB // 2
    padded = full * NB + jnp.where(short, NB // 2, NB)
    z = me // 8
    x = lax.rem(me // 2, 4)
    c = lax.rem(me, 2)

    def where_is(t):
        j = jnp.where(t < prompt, t, start + t - prompt)
        column = lax.rem(lax.rem(j, 2) + c, 2) * 4 + lax.rem(x - lax.rem(j // 2, 4) + 4, 4)
        return column, lax.rem(z - j // 8 + 4, 4)

    for zz in range(4):
        sz = lax.rem(z + 4 - zz, 4)
        for nb, buf in enumerate(bufs):
            j = zz * 8 + lax.rem(x + 4 - nb % 4, 4) * 2 + lax.rem(c + nb // 4, 2)
            t = jnp.where(j < prompt, j, j - start + prompt)

            @pl.when(live & (j <= me) & ((j < prompt) | (j >= start)))
            def _(buf=buf, sz=sz, t=t):
                pltpu.make_async_copy(buf.at[sz], kv.at[t], sem.at[t]).start()

    for h in range(GROUP):
        at = slice(h * DH, (h + 1) * DH)
        q2[h * BLOCK : (h + 1) * BLOCK, :] = q_ref[:, at]
        g2[h * BLOCK : (h + 1) * BLOCK, :] = do_ref[:, at]
    keep_ref[...] = jnp.zeros_like(keep_ref)
    send_ref[...] = jnp.zeros_like(send_ref)
    mx[...] = jnp.full_like(mx, -1e30)
    sm[...] = jnp.zeros_like(sm)
    dl[...] = jnp.zeros_like(dl)
    acc[...] = jnp.zeros_like(acc)

    def pad(t, _):
        kv[t] = jnp.zeros((2 * BLOCK, DH), bf)
        return 0

    lax.fori_loop(n, jnp.where(live, padded, 0), pad, 0)

    def land(t, _):
        pltpu.make_async_copy(bufs[0].at[0], kv.at[t], sem.at[t]).wait()
        return 0

    def part_of(i, kvi, blocks):
        part = kv[pl.ds(i * NB, blocks), kvi * BLOCK : (kvi + 1) * BLOCK, :]
        return part.reshape(blocks * BLOCK, DH)

    def forward(i, blocks, masked):
        keys = blocks * BLOCK
        rows = pl.ds(pl.multiple_of(i * KC, KC), keys)
        lax.fori_loop(i * NB, jnp.minimum(i * NB + blocks, n), land, 0)
        s = lax.dot_general(part_of(i, 0, blocks), q2[...], NT, preferred_element_type=f32) * c2
        if masked:
            key = lax.broadcasted_iota(jnp.int32, (keys, ROWS), 0) + i * KC - (n - 1) * BLOCK
            query = lax.rem(lax.broadcasted_iota(jnp.int32, (keys, ROWS), 1), BLOCK)
            s = jnp.where(key <= query, s, -jnp.inf)
        old = mx[0:1, :]
        top = jnp.max(s.reshape(keys // 8, 8, ROWS), axis=0)
        new = jnp.maximum(old, jnp.max(top, axis=0, keepdims=True))
        p = jnp.exp2(s - new)
        dp = lax.dot_general(part_of(i, 1, blocks), g2[...], NT, preferred_element_type=f32)
        fade = jnp.exp2(old - new)
        sm[...] = sm[...] * fade + jnp.sum(p.reshape(keys // 8, 8, ROWS), axis=0)
        dl[...] = dl[...] * fade + jnp.sum((p * dp).reshape(keys // 8, 8, ROWS), axis=0)
        mx[0:1, :] = new
        mt[i, 0:1, :] = new
        pb[rows, :] = p.astype(bf)
        dp_s[rows, :] = dp

    def step(i, _):
        forward(i, NB, False)
        return 0

    lax.fori_loop(0, full, step, 0)

    @pl.when(live & short)
    def _():
        forward(full, NB // 2, True)

    @pl.when(live & jnp.logical_not(short))
    def _():
        forward(full, NB, True)

    @pl.when(live)
    def _():
        inv = 1.0 / jnp.sum(sm[...], axis=0, keepdims=True)
        dl[0:1, :] = jnp.sum(dl[...], axis=0, keepdims=True) * inv
        sm[0:1, :] = inv

    def backward(i, blocks):
        rows = pl.ds(pl.multiple_of(i * KC, KC), blocks * BLOCK)
        f = sm[0:1, :] * jnp.exp2(mt[i, 0:1, :] - mx[0:1, :])
        p = pb[rows, :].astype(f32) * f
        g = (p * (dp_s[rows, :] - dl[0:1, :])).astype(bf)
        dk = lax.dot_general(g, q2[...], NN, preferred_element_type=f32)
        dv = lax.dot_general(p.astype(bf), g2[...], NN, preferred_element_type=f32)
        acc[...] += lax.dot_general(part_of(i, 0, blocks).T, g, NN, preferred_element_type=f32)
        for u in range(blocks):
            t = i * NB + u
            b, sz = where_is(t)
            sx = lax.rem(b, 4)
            dk_u = (dk[u * BLOCK : (u + 1) * BLOCK] * scale).astype(bf)
            dv_u = dv[u * BLOCK : (u + 1) * BLOCK].astype(bf)
            for crel, out in enumerate((keep_ref, send_ref)):

                @pl.when((t < n) & (b // 4 == crel))
                def _(out=out):
                    out[sx, sz, 0] = dk_u
                    out[sx, sz, 1] = dv_u

    def back_step(i, _):
        backward(i, NB)
        return 0

    whole = full + jnp.where(live & jnp.logical_not(short), 1, 0)
    lax.fori_loop(0, whole, back_step, 0)

    @pl.when(live & short)
    def _():
        backward(full, NB // 2)

    for h in range(GROUP):
        at = slice(h * BLOCK, (h + 1) * BLOCK)
        dq_ref[:, at] = (acc[:, at] * scale).T


def attend(bounds, q, do, bufs):
    nb = len(bufs)

    def kern(*refs):
        attend_body(refs[0], refs[1], refs[2], refs[3 : 3 + nb], *refs[3 + nb :])

    partial = jax.ShapeDtypeStruct((4, 4, 2, BLOCK, DH), bf)
    return pl.pallas_call(
        kern,
        out_shape=(jax.ShapeDtypeStruct((BLOCK, ROWS), f32), partial, partial),
        in_specs=[S, V, V] + [A] * nb,
        out_specs=(V, V, V),
        scratch_shapes=[
            pltpu.VMEM((32, 2 * BLOCK, DH), bf),
            pltpu.VMEM((ROWS, DH), bf),
            pltpu.VMEM((ROWS, DH), bf),
            pltpu.VMEM((32 * BLOCK, ROWS), bf),
            pltpu.VMEM((32 * BLOCK, ROWS), f32),
            pltpu.VMEM((32 // NB, 8, ROWS), f32),
            pltpu.VMEM((8, ROWS), f32),
            pltpu.VMEM((8, ROWS), f32),
            pltpu.VMEM((8, ROWS), f32),
            pltpu.VMEM((DH, ROWS), f32),
            pltpu.SemaphoreType.DMA((32,)),
        ],
        compiler_params=pltpu.CompilerParams(vmem_limit_bytes=36 * 2**20),
        cost_estimate=pl.CostEstimate(
            flops=10**10, bytes_accessed=5 * 2**20, transcendentals=2**22
        ),
    )(bounds, q, do, *bufs)

PAIRS = 8
SMALL = pltpu.CompilerParams(vmem_limit_bytes=8 * 2**20)


def seq_perm(move):
    pairs = []
    for z in range(4):
        for x in range(4):
            for c in range(2):
                nz, nx, nc = move(z, x, c)
                pairs.append(((z * 4 + x) * 2 + c, (nz * 4 + nx) * 2 + nc))
    return pairs


CORE = seq_perm(lambda z, x, c: (z, x, 1 - c))
X_UP = [seq_perm(lambda z, x, c, s=s: (z, (x + s) % 4, c)) for s in range(4)]
X_DOWN = [seq_perm(lambda z, x, c, s=s: (z, (x - s) % 4, c)) for s in range(4)]
Z_UP = [seq_perm(lambda z, x, c, s=s: ((z + s) % 4, x, c)) for s in range(4)]
Z_DOWN = [[(i, i - 8 * s) for i in range(8 * s, 32)] for s in range(4)]


HEAD_Y = [[(h, h // 4 * 4 + m[h % 4]) for h in range(8)] for m in ((1, 0, 3, 2), (3, 2, 1, 0))]
X_FLIP = [seq_perm(lambda z, x, c, m=m: (z, m[x], c)) for m in ((1, 0, 3, 2), (3, 2, 1, 0))]
HALVES = []
for seq_at in range(32):
    for head_at in range(8):
        far = (head_at // 4 * 4 + seq_at // 8) ^ 6
        HALVES.append(
            (seq_at * 8 + head_at, (far % 4 * 8 + seq_at % 8) * 8 + far // 4 * 4 + head_at % 4)
        )


def pack(keys, values, ratios):
    def kern(k_ref, v_ref, ratio_ref, out_ref):
        total = ratio_ref[0]
        for t in range(1, ratios.shape[0]):
            total = total + ratio_ref[t]
        whole = jnp.full((16, DH), total, f32)
        hi = whole.astype(bf).astype(f32)
        mid = (whole - hi).astype(bf).astype(f32)
        low = whole - hi - mid
        row = lax.broadcasted_iota(jnp.int32, (16, DH), 0)
        ride = jnp.where(row == 0, hi, jnp.where(row == 1, mid, jnp.where(row == 2, low, 0.0)))
        out_ref[:BLOCK, :] = k_ref[...]
        out_ref[BLOCK : 2 * BLOCK, :] = v_ref[...]
        out_ref[2 * BLOCK :, :] = ride.astype(bf)

    return pl.pallas_call(
        kern,
        out_shape=jax.ShapeDtypeStruct((2 * BLOCK + 16, DH), bf),
        in_specs=[V, V, S],
        out_specs=V,
    )(keys, values, ratios)


def block_sums(bounds, total, packets):
    def kern(b_ref, total_ref, p1, p2, p3, sums_ref, rides, sem):
        copies = [
            pltpu.make_async_copy(p.at[pl.ds(2 * BLOCK, 16)], rides.at[k], sem.at[k])
            for k, p in enumerate((p1, p2, p3))
        ]
        for copy in copies:
            copy.start()
        me = lax.axis_index("seq")
        row = lax.broadcasted_iota(jnp.int32, (RESP, DH), 0)
        part = total_ref[0:1, :]
        sums = jnp.zeros((RESP, DH), f32)
        for s in range(4):
            first = (lax.rem(me // 8 - s + 4, 4) * 8 + lax.rem(me, 8)) * BLOCK
            resp = jnp.int32(-1)
            for r in range(RESP):
                resp = resp + (first >= b_ref[r]).astype(jnp.int32)
            if s:
                copies[s - 1].wait()
                part = jnp.sum(rides[s - 1].astype(f32), axis=0, keepdims=True)
            sums = sums + jnp.where(row == resp, part, 0.0)
        sums_ref[...] = sums

    return pl.pallas_call(
        kern,
        out_shape=jax.ShapeDtypeStruct((RESP, DH), f32),
        in_specs=[S, V, A, A, A],
        out_specs=V,
        scratch_shapes=[pltpu.VMEM((3, 16, DH), bf), pltpu.SemaphoreType.DMA((3,))],
        compiler_params=SMALL,
    )(bounds, total, *packets)


def live_planes(b_ref, z):
    prompt = b_ref[0] // BLOCK
    start = jnp.int32(0)
    for r in range(RESP):
        lo = b_ref[r] // BLOCK
        start = jnp.where(z * 8 >= lo, lo, start)

    def live(plane, column):
        j = plane * 8 + column
        return (plane < z) & ((j < prompt) | ((z * 8 >= prompt) & (j >= start)))

    return live


def small_things(bounds, ratios):
    def kern(b_ref, ratio_ref, out_ref, total_ref):
        most = jnp.int32(0)
        for z in range(1, 4):
            live = live_planes(b_ref, jnp.int32(z))
            for column in range(8):
                count = jnp.int32(0)
                for plane in range(z):
                    count = count + live(jnp.int32(plane), column).astype(jnp.int32)
                most = jnp.maximum(most, count)
        out_ref[0] = most + 1
        total = ratio_ref[0]
        for t in range(1, ratios.shape[0]):
            total = total + ratio_ref[t]
        total_ref[...] = jnp.full(total_ref.shape, total, f32)

    return pl.pallas_call(
        kern,
        out_shape=(
            jax.ShapeDtypeStruct((1,), jnp.int32),
            jax.ShapeDtypeStruct((8, DH), f32),
        ),
        in_specs=[S, S],
        out_specs=(S, V),
        compiler_params=SMALL,
    )(bounds, ratios)


def core_add(slots, sums, table, keep, got):
    def kern(sums_ref, b_ref, keep_ref, got_ref, o0, o1, o2, o3, w_ref, mean, coef):
        me = lax.axis_index("seq")
        for r in range(RESP):
            mean[r] = sums_ref[r, 0] / (b_ref[r + 1] - b_ref[r]).astype(f32)
            coef[r] = 0.0
        for p in range(PAIRS):
            win, lose = b_ref[RESP + 1 + 2 * p], b_ref[RESP + 2 + 2 * p]
            resid = mean[win] - mean[lose] - 1.0
            coef[win] = coef[win] + resid
            coef[lose] = coef[lose] - resid

        def weight(block):
            first = block * BLOCK
            w = jnp.float32(0.0)
            for r in range(RESP):
                inside = (first >= b_ref[r]) & (first < b_ref[r + 1])
                length = (b_ref[r + 1] - b_ref[r]).astype(f32)
                w = jnp.where(inside, 512.0 * (2.0 / PAIRS * coef[r] / length), w)
            return w

        mine = weight(me)
        theirs = weight(me + 1 - 2 * lax.rem(me, 2))
        w_ref[...] = jnp.full(w_ref.shape, mine, f32)
        z = me // 8
        live = live_planes(b_ref, z)
        for sx, out in enumerate((o0, o1, o2, o3)):
            column = lax.rem(me // 2 - sx + 4, 4) * 2 + lax.rem(me, 2)

            def fill(slot, sz, sx=sx, out=out):
                for kvi in range(2):
                    out[slot, kvi] = (
                        keep_ref[sx, sz, kvi].astype(f32) * mine
                        + got_ref[sx, sz, kvi].astype(f32) * theirs
                    ).astype(bf)

            fill(0, 0)
            slot = jnp.int32(1)
            for plane in range(3):
                used = live(jnp.int32(plane), column)

                @pl.when(used)
                def _(slot=slot, plane=plane, fill=fill):
                    fill(slot, z - plane)

                slot = slot + used.astype(jnp.int32)

    slot = jax.ShapeDtypeStruct((slots, 2, 128, 128), bf)
    return pl.pallas_call(
        kern,
        out_shape=(slot, slot, slot, slot, jax.ShapeDtypeStruct((8, ROWS), f32)),
        in_specs=[S, S, V, V],
        out_specs=(V,) * 5,
        scratch_shapes=[pltpu.SMEM((RESP,), f32), pltpu.SMEM((RESP,), f32)],
        compiler_params=SMALL,
    )(sums, table, keep, got)


def x_add(bounds, parts):
    def kern(b_ref, i0, i1, i2, i3, *outs):
        me = lax.axis_index("seq")
        z = me // 8
        live = live_planes(b_ref, z)
        used = [live(jnp.int32(plane), lax.rem(me, 8)).astype(jnp.int32) for plane in range(3)]

        def total(slot, kvi):
            return (
                (i0[slot, kvi].astype(f32) + i1[slot, kvi].astype(f32))
                + (i2[slot, kvi].astype(f32) + i3[slot, kvi].astype(f32))
            ).astype(bf)

        for kvi in range(2):
            outs[0][kvi] = total(0, kvi)
        for sz in range(1, 4):
            plane = z - sz
            slot = 1 + jnp.where(plane > 0, used[0], 0) + jnp.where(plane > 1, used[1], 0)
            here = jnp.int32(0)
            for p in range(3):
                here = jnp.where(plane == p, used[p], here)

            @pl.when(here == 1)
            def _(sz=sz, slot=slot):
                for kvi in range(2):
                    outs[sz][kvi] = total(slot, kvi)

            @pl.when(here == 0)
            def _(sz=sz):
                outs[sz][...] = jnp.zeros_like(outs[sz])

    slot = jax.ShapeDtypeStruct((2, 128, 128), bf)
    return pl.pallas_call(
        kern,
        out_shape=(slot,) * 4,
        in_specs=[S] + [V] * 4,
        out_specs=(V,) * 4,
        compiler_params=SMALL,
    )(bounds, *parts)


def z_add(a0, a1, a2, a3):
    def kern(i0, i1, i2, i3, dk, dv):
        for kvi, out in enumerate((dk, dv)):
            out[...] = (
                (i0[kvi].astype(f32) + i1[kvi].astype(f32))
                + (i2[kvi].astype(f32) + i3[kvi].astype(f32))
            ).astype(bf)

    out = jax.ShapeDtypeStruct((BLOCK, DH), bf)
    return pl.pallas_call(
        kern,
        out_shape=(out, out),
        in_specs=[V] * 4,
        out_specs=(V, V),
        compiler_params=SMALL,
    )(a0, a1, a2, a3)


def shards(query_rows, key_rows, value_rows, out_grad, log_ratio, block_mask, bounds, pairs):
    def seq(v, perm):
        return lax.ppermute(v, "seq", perm)

    packet = pack(key_rows, value_rows, log_ratio)
    by_z = [packet] + [seq(packet, Z_UP[s]) for s in (1, 2, 3)]
    table = jnp.concatenate([bounds, pairs.reshape(2 * PAIRS)])
    slots, total = small_things(table, log_ratio)
    moved, table, total, slots = lax.optimization_barrier((by_z[1:], table, total, slots))
    by_z = [packet] + moved
    column = jnp.stack([p[: 2 * BLOCK] for p in by_z])
    column, moved = lax.optimization_barrier((column, moved))
    far = seq(column, X_UP[2])
    sums, column = lax.optimization_barrier((block_sums(table, total, moved), column))
    turned = lax.ppermute(sums, "heads", HEAD_Y[0])
    before = seq(column, X_UP[1])
    sums, column = lax.optimization_barrier((sums + turned, column))
    turned = lax.ppermute(sums, "heads", HEAD_Y[1])
    after = seq(column, X_UP[3])
    sums = sums + turned
    by_x = [column, before, far, after]
    sums = sums + lax.ppermute(sums, ("seq", "heads"), HALVES)
    sums, by_x = lax.optimization_barrier((sums, by_x))
    bufs = by_x + [seq(b, CORE) for b in by_x]
    sums = sums + seq(sums, CORE)
    sums, bufs = lax.optimization_barrier((sums, bufs))
    turned = seq(sums, X_FLIP[0])
    dq, keep, send = attend(table, query_rows, out_grad, bufs)
    sums, send = lax.optimization_barrier((sums + turned, send))
    got = seq(send, CORE)
    sums = sums + seq(sums, X_FLIP[1])

    def across_x(slots):
        def branch(sums, keep, got):
            *by_shift, weight = core_add(slots, sums, table, keep, got)
            far = seq(by_shift[2], X_DOWN[2])
            near = [seq(by_shift[s], X_DOWN[s]) for s in (1, 3)]
            return x_add(table, [by_shift[0], far] + near), weight

        return branch

    summed, weight = lax.switch(
        slots[0] - 2, [across_x(2), across_x(3), across_x(4)], sums, keep, got
    )
    query_grad = (dq * weight[:1]).astype(bf)
    key_grad, value_grad = z_add(summed[0], *[seq(summed[s], Z_DOWN[s]) for s in (3, 2, 1)])
    return query_grad, key_grad, value_grad


def solution(mesh):
    whole = P("seq", "heads")
    return jax.shard_map(
        shards,
        mesh=mesh,
        in_specs=(whole, whole, whole, whole, P(("seq", "heads")), P(), P(), P()),
        out_specs=(whole, whole, whole),
        check_vma=False,
    )
```

```python
import math

import jax
import jax.numpy as jnp
from jax import lax
from jax.experimental import pallas as pl
from jax.experimental.pallas import tpu as pltpu
from jax.sharding import PartitionSpec as P

DH = 128
BLOCK = 128
RESP = 8
GROUP = 8
ROWS = GROUP * BLOCK
PACKET = 2 * BLOCK + 16
NB = 4
KC = NB * BLOCK
scale = 1.0 / math.sqrt(DH)
c2 = scale * math.log2(math.e)
f32 = jnp.float32
bf = jnp.bfloat16
NT = (((1,), (1,)), ((), ()))
NN = (((1,), (0,)), ((), ()))
S = pl.BlockSpec(memory_space=pltpu.SMEM)
V = pl.BlockSpec(memory_space=pltpu.VMEM)
A = pl.BlockSpec(memory_space=pl.ANY)


def attend_body(
    bounds, q_ref, do_ref, bufs, dq_ref, keep_ref, send_ref,
    kv, q2, g2, pb, dp_s, mt, mx, sm, dl, acc, sem,
):
    me = lax.axis_index("seq")
    prompt = bounds[0] // BLOCK
    start = jnp.int32(0)
    for r in range(RESP):
        lo = bounds[r] // BLOCK
        start = jnp.where(me >= lo, lo, start)
    live = me >= prompt
    n = jnp.where(live, prompt + me - start + 1, 0)
    full = jnp.maximum(n - 1, 0) // NB
    short = n - full * NB <= NB // 2
    padded = full * NB + jnp.where(short, NB // 2, NB)
    z = me // 8
    x = lax.rem(me // 2, 4)
    c = lax.rem(me, 2)

    def where_is(t):
        j = jnp.where(t < prompt, t, start + t - prompt)
        column = lax.rem(lax.rem(j, 2) + c, 2) * 4 + lax.rem(x - lax.rem(j // 2, 4) + 4, 4)
        return column, lax.rem(z - j // 8 + 4, 4)

    for zz in range(4):
        sz = lax.rem(z + 4 - zz, 4)
        for nb, buf in enumerate(bufs):
            j = zz * 8 + lax.rem(x + 4 - nb % 4, 4) * 2 + lax.rem(c + nb // 4, 2)
            t = jnp.where(j < prompt, j, j - start + prompt)

            @pl.when(live & (j <= me) & ((j < prompt) | (j >= start)))
            def _(buf=buf, sz=sz, t=t):
                pltpu.make_async_copy(buf.at[sz], kv.at[t], sem.at[t]).start()

    for h in range(GROUP):
        at = slice(h * DH, (h + 1) * DH)
        q2[h * BLOCK : (h + 1) * BLOCK, :] = q_ref[:, at]
        g2[h * BLOCK : (h + 1) * BLOCK, :] = do_ref[:, at]
    keep_ref[...] = jnp.zeros_like(keep_ref)
    send_ref[...] = jnp.zeros_like(send_ref)
    mx[...] = jnp.full_like(mx, -1e30)
    sm[...] = jnp.zeros_like(sm)
    dl[...] = jnp.zeros_like(dl)
    acc[...] = jnp.zeros_like(acc)

    def pad(t, _):
        kv[t] = jnp.zeros((2 * BLOCK, DH), bf)
        return 0

    lax.fori_loop(n, jnp.where(live, padded, 0), pad, 0)

    def land(t, _):
        pltpu.make_async_copy(bufs[0].at[0], kv.at[t], sem.at[t]).wait()
        return 0

    def part_of(i, kvi, blocks):
        part = kv[pl.ds(i * NB, blocks), kvi * BLOCK : (kvi + 1) * BLOCK, :]
        return part.reshape(blocks * BLOCK, DH)

    def forward(i, blocks, masked):
        keys = blocks * BLOCK
        rows = pl.ds(pl.multiple_of(i * KC, KC), keys)
        lax.fori_loop(i * NB, jnp.minimum(i * NB + blocks, n), land, 0)
        s = lax.dot_general(part_of(i, 0, blocks), q2[...], NT, preferred_element_type=f32) * c2
        if masked:
            key = lax.broadcasted_iota(jnp.int32, (keys, ROWS), 0) + i * KC - (n - 1) * BLOCK
            query = lax.rem(lax.broadcasted_iota(jnp.int32, (keys, ROWS), 1), BLOCK)
            s = jnp.where(key <= query, s, -jnp.inf)
        old = mx[0:1, :]
        top = jnp.max(s.reshape(keys // 8, 8, ROWS), axis=0)
        new = jnp.maximum(old, jnp.max(top, axis=0, keepdims=True))
        p = jnp.exp2(s - new)
        dp = lax.dot_general(part_of(i, 1, blocks), g2[...], NT, preferred_element_type=f32)
        fade = jnp.exp2(old - new)
        sm[...] = sm[...] * fade + jnp.sum(p.reshape(keys // 8, 8, ROWS), axis=0)
        dl[...] = dl[...] * fade + jnp.sum((p * dp).reshape(keys // 8, 8, ROWS), axis=0)
        mx[0:1, :] = new
        mt[i, 0:1, :] = new
        pb[rows, :] = p.astype(bf)
        dp_s[rows, :] = dp

    def step(i, _):
        forward(i, NB, False)
        return 0

    lax.fori_loop(0, full, step, 0)

    @pl.when(live & short)
    def _():
        forward(full, NB // 2, True)

    @pl.when(live & jnp.logical_not(short))
    def _():
        forward(full, NB, True)

    @pl.when(live)
    def _():
        inv = 1.0 / jnp.sum(sm[...], axis=0, keepdims=True)
        dl[0:1, :] = jnp.sum(dl[...], axis=0, keepdims=True) * inv
        sm[0:1, :] = inv

    def backward(i, blocks):
        rows = pl.ds(pl.multiple_of(i * KC, KC), blocks * BLOCK)
        f = sm[0:1, :] * jnp.exp2(mt[i, 0:1, :] - mx[0:1, :])
        p = pb[rows, :].astype(f32) * f
        g = (p * (dp_s[rows, :] - dl[0:1, :])).astype(bf)
        dk = lax.dot_general(g, q2[...], NN, preferred_element_type=f32)
        dv = lax.dot_general(p.astype(bf), g2[...], NN, preferred_element_type=f32)
        acc[...] += lax.dot_general(part_of(i, 0, blocks).T, g, NN, preferred_element_type=f32)
        for u in range(blocks):
            t = i * NB + u
            b, sz = where_is(t)
            sx = lax.rem(b, 4)
            dk_u = (dk[u * BLOCK : (u + 1) * BLOCK] * scale).astype(bf)
            dv_u = dv[u * BLOCK : (u + 1) * BLOCK].astype(bf)
            for crel, out in enumerate((keep_ref, send_ref)):

                @pl.when((t < n) & (b // 4 == crel))
                def _(out=out):
                    out[sx, sz, 0] = dk_u
                    out[sx, sz, 1] = dv_u

    def back_step(i, _):
        backward(i, NB)
        return 0

    whole = full + jnp.where(live & jnp.logical_not(short), 1, 0)
    lax.fori_loop(0, whole, back_step, 0)

    @pl.when(live & short)
    def _():
        backward(full, NB // 2)

    for h in range(GROUP):
        at = slice(h * BLOCK, (h + 1) * BLOCK)
        dq_ref[:, at] = (acc[:, at] * scale).T


def attend(bounds, q, do, bufs):
    nb = len(bufs)

    def kern(*refs):
        attend_body(refs[0], refs[1], refs[2], refs[3 : 3 + nb], *refs[3 + nb :])

    partial = jax.ShapeDtypeStruct((4, 4, 2, BLOCK, DH), bf)
    return pl.pallas_call(
        kern,
        out_shape=(jax.ShapeDtypeStruct((BLOCK, ROWS), f32), partial, partial),
        in_specs=[S, V, V] + [A] * nb,
        out_specs=(V, V, V),
        scratch_shapes=[
            pltpu.VMEM((32, 2 * BLOCK, DH), bf),
            pltpu.VMEM((ROWS, DH), bf),
            pltpu.VMEM((ROWS, DH), bf),
            pltpu.VMEM((32 * BLOCK, ROWS), bf),
            pltpu.VMEM((32 * BLOCK, ROWS), f32),
            pltpu.VMEM((32 // NB, 8, ROWS), f32),
            pltpu.VMEM((8, ROWS), f32),
            pltpu.VMEM((8, ROWS), f32),
            pltpu.VMEM((8, ROWS), f32),
            pltpu.VMEM((DH, ROWS), f32),
            pltpu.SemaphoreType.DMA((32,)),
        ],
        compiler_params=pltpu.CompilerParams(vmem_limit_bytes=36 * 2**20),
        cost_estimate=pl.CostEstimate(
            flops=10**10, bytes_accessed=5 * 2**20, transcendentals=2**22
        ),
    )(bounds, q, do, *bufs)

PAIRS = 8
SMALL = pltpu.CompilerParams(vmem_limit_bytes=8 * 2**20)


def seq_perm(move):
    pairs = []
    for z in range(4):
        for x in range(4):
            for c in range(2):
                nz, nx, nc = move(z, x, c)
                pairs.append(((z * 4 + x) * 2 + c, (nz * 4 + nx) * 2 + nc))
    return pairs


CORE = seq_perm(lambda z, x, c: (z, x, 1 - c))
X_UP = [seq_perm(lambda z, x, c, s=s: (z, (x + s) % 4, c)) for s in range(4)]
X_DOWN = [seq_perm(lambda z, x, c, s=s: (z, (x - s) % 4, c)) for s in range(4)]
Z_UP = [seq_perm(lambda z, x, c, s=s: ((z + s) % 4, x, c)) for s in range(4)]
Z_DOWN = [[(i, i - 8 * s) for i in range(8 * s, 32)] for s in range(4)]


HEAD_Y = [[(h, h // 4 * 4 + m[h % 4]) for h in range(8)] for m in ((1, 0, 3, 2), (3, 2, 1, 0))]
X_FLIP = [seq_perm(lambda z, x, c, m=m: (z, m[x], c)) for m in ((1, 0, 3, 2), (3, 2, 1, 0))]
HALVES = []
for seq_at in range(32):
    for head_at in range(8):
        far = (head_at // 4 * 4 + seq_at // 8) ^ 6
        HALVES.append(
            (seq_at * 8 + head_at, (far % 4 * 8 + seq_at % 8) * 8 + far // 4 * 4 + head_at % 4)
        )


def pack(keys, values, ratios):
    def kern(k_ref, v_ref, ratio_ref, out_ref):
        total = ratio_ref[0]
        for t in range(1, ratios.shape[0]):
            total = total + ratio_ref[t]
        whole = jnp.full((16, DH), total, f32)
        hi = whole.astype(bf).astype(f32)
        mid = (whole - hi).astype(bf).astype(f32)
        low = whole - hi - mid
        row = lax.broadcasted_iota(jnp.int32, (16, DH), 0)
        ride = jnp.where(row == 0, hi, jnp.where(row == 1, mid, jnp.where(row == 2, low, 0.0)))
        out_ref[:BLOCK, :] = k_ref[...]
        out_ref[BLOCK : 2 * BLOCK, :] = v_ref[...]
        out_ref[2 * BLOCK :, :] = ride.astype(bf)

    return pl.pallas_call(
        kern,
        out_shape=jax.ShapeDtypeStruct((2 * BLOCK + 16, DH), bf),
        in_specs=[V, V, S],
        out_specs=V,
    )(keys, values, ratios)


def block_sums(bounds, total, packets):
    def kern(b_ref, total_ref, p1, p2, p3, sums_ref, rides, sem):
        copies = [
            pltpu.make_async_copy(p.at[pl.ds(2 * BLOCK, 16)], rides.at[k], sem.at[k])
            for k, p in enumerate((p1, p2, p3))
        ]
        for copy in copies:
            copy.start()
        me = lax.axis_index("seq")
        row = lax.broadcasted_iota(jnp.int32, (RESP, DH), 0)
        part = total_ref[0:1, :]
        sums = jnp.zeros((RESP, DH), f32)
        for s in range(4):
            first = (lax.rem(me // 8 - s + 4, 4) * 8 + lax.rem(me, 8)) * BLOCK
            resp = jnp.int32(-1)
            for r in range(RESP):
                resp = resp + (first >= b_ref[r]).astype(jnp.int32)
            if s:
                copies[s - 1].wait()
                part = jnp.sum(rides[s - 1].astype(f32), axis=0, keepdims=True)
            sums = sums + jnp.where(row == resp, part, 0.0)
        sums_ref[...] = sums

    return pl.pallas_call(
        kern,
        out_shape=jax.ShapeDtypeStruct((RESP, DH), f32),
        in_specs=[S, V, A, A, A],
        out_specs=V,
        scratch_shapes=[pltpu.VMEM((3, 16, DH), bf), pltpu.SemaphoreType.DMA((3,))],
        compiler_params=SMALL,
    )(bounds, total, *packets)


def live_planes(b_ref, z):
    prompt = b_ref[0] // BLOCK
    start = jnp.int32(0)
    for r in range(RESP):
        lo = b_ref[r] // BLOCK
        start = jnp.where(z * 8 >= lo, lo, start)

    def live(plane, column):
        j = plane * 8 + column
        return (plane < z) & ((j < prompt) | ((z * 8 >= prompt) & (j >= start)))

    return live


def small_things(bounds, ratios):
    def kern(b_ref, ratio_ref, out_ref, total_ref):
        most = jnp.int32(0)
        for z in range(1, 4):
            live = live_planes(b_ref, jnp.int32(z))
            for column in range(8):
                count = jnp.int32(0)
                for plane in range(z):
                    count = count + live(jnp.int32(plane), column).astype(jnp.int32)
                most = jnp.maximum(most, count)
        out_ref[0] = most + 1
        total = ratio_ref[0]
        for t in range(1, ratios.shape[0]):
            total = total + ratio_ref[t]
        total_ref[...] = jnp.full(total_ref.shape, total, f32)

    return pl.pallas_call(
        kern,
        out_shape=(
            jax.ShapeDtypeStruct((1,), jnp.int32),
            jax.ShapeDtypeStruct((8, DH), f32),
        ),
        in_specs=[S, S],
        out_specs=(S, V),
        compiler_params=SMALL,
    )(bounds, ratios)


def core_add(slots, sums, table, keep, got):
    def kern(sums_ref, b_ref, keep_ref, got_ref, o0, o1, o2, o3, w_ref, m_ref, mean, coef):
        me = lax.axis_index("seq")
        for r in range(RESP):
            mean[r] = sums_ref[r, 0] / (b_ref[r + 1] - b_ref[r]).astype(f32)
            coef[r] = 0.0
        for p in range(PAIRS):
            win, lose = b_ref[RESP + 1 + 2 * p], b_ref[RESP + 2 + 2 * p]
            resid = mean[win] - mean[lose] - 1.0
            coef[win] = coef[win] + resid
            coef[lose] = coef[lose] - resid

        def weight(block):
            first = block * BLOCK
            w = jnp.float32(0.0)
            for r in range(RESP):
                inside = (first >= b_ref[r]) & (first < b_ref[r + 1])
                length = (b_ref[r + 1] - b_ref[r]).astype(f32)
                w = jnp.where(inside, 512.0 * (2.0 / PAIRS * coef[r] / length), w)
            return w

        mine = weight(me)
        theirs = weight(me + 1 - 2 * lax.rem(me, 2))
        w_ref[...] = jnp.full(w_ref.shape, mine, f32)
        z = me // 8
        live = live_planes(b_ref, z)
        own = [live(jnp.int32(plane), lax.rem(me, 8)).astype(jnp.int32) for plane in range(3)]
        place = [jnp.int32(1), 1 + own[0], 1 + own[0] + own[1]]
        for sz in range(1, 4):
            for k in range(1, slots):
                flag = jnp.int32(0)
                for plane in range(3):
                    flag = jnp.where((z - plane == sz) & (place[plane] == k), own[plane], flag)
                m_ref[sz - 1, k - 1] = jnp.full((8, DH), flag, jnp.int32)
        for sx, out in enumerate((o0, o1, o2, o3)):
            column = lax.rem(me // 2 - sx + 4, 4) * 2 + lax.rem(me, 2)

            def fill(slot, sz, sx=sx, out=out):
                for kvi in range(2):
                    out[slot, kvi] = (
                        keep_ref[sx, sz, kvi].astype(f32) * mine
                        + got_ref[sx, sz, kvi].astype(f32) * theirs
                    ).astype(bf)

            fill(0, 0)
            slot = jnp.int32(1)
            for plane in range(3):
                used = live(jnp.int32(plane), column)

                @pl.when(used)
                def _(slot=slot, plane=plane, fill=fill):
                    fill(slot, z - plane)

                slot = slot + used.astype(jnp.int32)

    slot = jax.ShapeDtypeStruct((slots, 2, 128, 128), bf)
    return pl.pallas_call(
        kern,
        out_shape=(slot, slot, slot, slot, jax.ShapeDtypeStruct((8, ROWS), f32), jax.ShapeDtypeStruct((3, slots - 1, 8, DH), jnp.int32)),
        in_specs=[S, S, V, V],
        out_specs=(V,) * 6,
        scratch_shapes=[pltpu.SMEM((RESP,), f32), pltpu.SMEM((RESP,), f32)],
        compiler_params=SMALL,
    )(sums, table, keep, got)


def x_add(slots, masks, parts):
    def kern(m_ref, i0, i1, i2, i3, *outs):
        for kvi in range(2):
            totals = [
                (i0[k, kvi].astype(f32) + i1[k, kvi].astype(f32))
                + (i2[k, kvi].astype(f32) + i3[k, kvi].astype(f32))
                for k in range(slots)
            ]
            outs[0][kvi] = totals[0].astype(bf)
            for sz in range(1, 4):
                picked = jnp.zeros((BLOCK, DH), f32)
                for k in range(1, slots):
                    picked = jnp.where(m_ref[sz - 1, k - 1][0:1, :] > 0, totals[k], picked)
                outs[sz][kvi] = picked.astype(bf)

    slot = jax.ShapeDtypeStruct((2, 128, 128), bf)
    return pl.pallas_call(
        kern,
        out_shape=(slot,) * 4,
        in_specs=[V] * 5,
        out_specs=(V,) * 4,
        compiler_params=SMALL,
    )(masks, *parts)


def z_add(a0, a1, a2, a3):
    def kern(i0, i1, i2, i3, dk, dv):
        for kvi, out in enumerate((dk, dv)):
            out[...] = (
                (i0[kvi].astype(f32) + i1[kvi].astype(f32))
                + (i2[kvi].astype(f32) + i3[kvi].astype(f32))
            ).astype(bf)

    out = jax.ShapeDtypeStruct((BLOCK, DH), bf)
    return pl.pallas_call(
        kern,
        out_shape=(out, out),
        in_specs=[V] * 4,
        out_specs=(V, V),
        compiler_params=SMALL,
    )(a0, a1, a2, a3)


def shards(query_rows, key_rows, value_rows, out_grad, log_ratio, block_mask, bounds, pairs):
    def seq(v, perm):
        return lax.ppermute(v, "seq", perm)

    packet = pack(key_rows, value_rows, log_ratio)
    by_z = [packet] + [seq(packet, Z_UP[s]) for s in (1, 2, 3)]
    table = jnp.concatenate([bounds, pairs.reshape(2 * PAIRS)])
    slots, total = small_things(table, log_ratio)
    moved, table, total, slots = lax.optimization_barrier((by_z[1:], table, total, slots))
    by_z = [packet] + moved
    column = jnp.stack([p[: 2 * BLOCK] for p in by_z])
    column, moved = lax.optimization_barrier((column, moved))
    far = seq(column, X_UP[2])
    sums, column = lax.optimization_barrier((block_sums(table, total, moved), column))
    turned = lax.ppermute(sums, "heads", HEAD_Y[0])
    before = seq(column, X_UP[1])
    sums, column = lax.optimization_barrier((sums + turned, column))
    turned = lax.ppermute(sums, "heads", HEAD_Y[1])
    after = seq(column, X_UP[3])
    sums = sums + turned
    by_x = [column, before, far, after]
    sums = sums + lax.ppermute(sums, ("seq", "heads"), HALVES)
    sums, by_x = lax.optimization_barrier((sums, by_x))
    bufs = by_x + [seq(b, CORE) for b in by_x]
    sums = sums + seq(sums, CORE)
    sums, bufs = lax.optimization_barrier((sums, bufs))
    turned = seq(sums, X_FLIP[0])
    dq, keep, send = attend(table, query_rows, out_grad, bufs)
    sums, send = lax.optimization_barrier((sums + turned, send))
    got = seq(send, CORE)
    sums = sums + seq(sums, X_FLIP[1])

    def across_x(slots):
        def branch(sums, keep, got):
            *by_shift, weight, masks = core_add(slots, sums, table, keep, got)
            far = seq(by_shift[2], X_DOWN[2])
            near = [seq(by_shift[s], X_DOWN[s]) for s in (1, 3)]
            return x_add(slots, masks, [by_shift[0], far] + near), weight

        return branch

    summed, weight = lax.switch(
        slots[0] - 2, [across_x(2), across_x(3), across_x(4)], sums, keep, got
    )
    query_grad = (dq * weight[:1]).astype(bf)
    key_grad, value_grad = z_add(summed[0], *[seq(summed[s], Z_DOWN[s]) for s in (3, 2, 1)])
    return query_grad, key_grad, value_grad


def solution(mesh):
    whole = P("seq", "heads")
    return jax.shard_map(
        shards,
        mesh=mesh,
        in_specs=(whole, whole, whole, whole, P(("seq", "heads")), P(), P(), P()),
        out_specs=(whole, whole, whole),
        check_vma=False,
    )
```
